256 devices in a mesh: clus: 64 (over z, y, core), rhs: 4 (over x).
Axes of the slice: x: 4, y: 4, z: 8, core: 2. Of those that a mesh axis runs over, the one named last changes fastest.
Arguments:
- vectors: bfloat16 [64, 262144], P('rhs', 'clus'), may hold values from -6 to 6
- near_field_tiles: bfloat16 [1024, 8, 256, 256], P('clus', 'rhs'), may hold values from -0.125 to 0.125
- near_lists: int32 [1024, 8], P('clus', 'rhs'), may hold values from 0 to 1023, as said below
- leaf_basis_set: bfloat16 [1024, 32, 256], P('clus'), may hold values from -0.375 to 0.375
- far_coupling: bfloat16 [1024, 32, 256], P('clus'), may hold values from -1 to 1
- far_device: int32 [1024, 8], P('clus'), may hold values from 0 to 63, all different within a row; in each aligned block of 16 rows (0 to 15, 16 to 31, ...) at most 4 rows name the same one
- far_leaf: int32 [1024, 8], P('clus'), may hold values from 0 to 15
- transfer: bfloat16 [1024, 32, 32], P('clus'), may hold values from -0.25 to 0.25
- parent: int32 [1024], P('clus'), may hold values from 0 to 63, as said below
- top_coupling: bfloat16 [2048, 2048], P('clus'), may hold values from -0.125 to 0.125
Outputs:
- first_product: bfloat16 [64, 262144], P('rhs', 'clus')
- second_product: bfloat16 [64, 262144], P('rhs', 'clus')
The draws below stay inside these ranges and needn't reach their ends.
Inputs may be any that keep to these rules, and one draw needn't show every extreme that they name: `near_lists`: entry [i, p] is a leaf at most 16 places from i in the cyclic order of leaves; in every draw some entry lies exactly 16 places below and some exactly 16 places above. `far_device`: each row names 8 different indices; among the rows of one device no index is named by more than 4 rows. `parent`: each top-level cluster holds 1 to 31 consecutive leaves, and one holds exactly that many; leaves 2 * k * 16 to 2 * (k + 1) * 16 - 1 belong to clusters (2 * k + 32) mod 64 and (2 * k + 1 + 64 / 2) mod 64.
All inputs are finite; a program needn't handle non-finite values.
Results may differ from the reference program's by a relative error of at most 0.012.
Values may be sent and summed in bfloat16 or wider, within the bound.
A program may use at most 64 MiB of HBM per device.

```python
import math
import jax
import jax.numpy as jnp
import numpy as np
from jax import lax

LEAF = 256
RANK = 32
NRHS = 64
L_DEV = 16
NEAR = 8
FAR = 8
NLEAF = 1024
UNKNOWNS = 262144
NTOP = 64
CAP = 4
N_CLUS = 64


def draw_near_lists(key, part):
    key = jax.random.fold_in(key, 7)
    leaf_rows = jnp.arange(NLEAF, dtype=jnp.int32)[:, None]
    column_ids = jnp.arange(NEAR, dtype=jnp.int32)[None, :]
    offset = jax.random.randint(key, (NLEAF, NEAR), -L_DEV, L_DEV + 1, dtype=jnp.int32)
    offset = jnp.where((leaf_rows == 0) & (column_ids == 0), -L_DEV, offset)
    offset = jnp.where((leaf_rows == 1) & (column_ids == 0), L_DEV, offset)
    return ((leaf_rows + offset + NLEAF) % NLEAF).astype(jnp.int32)


def draw_parent(key, part):
    key = jax.random.fold_in(key, 11)
    pair_count = NTOP // 2
    split_at = jax.random.randint(key, (pair_count,), 1, 2 * L_DEV, dtype=jnp.int32)
    split_at = split_at.at[0].set(1)
    leaf_ids = jnp.arange(NLEAF, dtype=jnp.int32)
    pair_ids = leaf_ids // (2 * L_DEV)
    inside = leaf_ids % (2 * L_DEV)
    second = (inside >= split_at[pair_ids]).astype(jnp.int32)
    cluster = 2 * pair_ids + second
    return ((cluster + NTOP // 2) % NTOP).astype(jnp.int32)


def place_ends(values, key, low, largest):
    place = [jax.random.randint(jax.random.fold_in(key, axis), (), 0, length) for axis, length in enumerate(values.shape)]
    longest = values.shape.index(max(values.shape))
    neighbour = place[:longest] + [(place[longest] + 1) % values.shape[longest]] + place[longest + 1:]
    return values.at[tuple(place)].set(low).at[tuple(neighbour)].set(largest)


def levels(rng, shape, shards, smallest, largest):
    gain = 1.0
    for position, blocks in shards:
        heights = jax.random.uniform(jax.random.fold_in(jax.random.fold_in(rng, 6), position), (blocks,), jnp.float32, smallest / len(shards), largest / len(shards))
        gain = gain * jnp.repeat(jnp.exp(heights), shape[position] // blocks).reshape((-1,) + (1,) * (len(shape) - 1 - position))
    return gain


def routed_block(own_key, own, number, rows, count, top, reach, slope):
    order = jax.random.permutation(own_key, count)
    packed, usual = shares(count, rows * top, reach, slope, True), shares(count, rows * top, reach, slope, False)
    places = jnp.arange(count)

    def named(tallies, turn):
        used = int((tallies > 0).sum())
        fixed = max(1, used // 4)
        passed = fixed + (places - fixed + turn * (used - fixed)) % max(1, count - fixed)
        return jnp.zeros((count,), jnp.int32).at[order[jnp.where(places < fixed, places, passed)]].set(jnp.asarray(tallies, jnp.int32))

    tallies = jnp.where(number % 4 == 0, named(packed, number // 4), named(usual, number - number // 4 - 1))
    mixed = jax.random.permutation(jax.random.fold_in(own, 3), count)
    giver, sink = mixed[0:count // 2 * 2:2], mixed[1:count // 2 * 2:2]
    margin = jnp.minimum(tallies[giver] - 1, reach - tallies[sink]) // 2
    margin = jnp.where((giver == order[0]) | (sink == order[0]) | (tallies[sink] == 0), 0, jnp.maximum(margin, 0))
    passed = jax.random.randint(jax.random.fold_in(own, 4), (count // 2,), 0, 1 << 20) % (margin + 1)
    tallies = tallies.at[giver].add(-passed).at[sink].add(passed)
    members = jnp.searchsorted(jnp.cumsum(tallies), jnp.arange(rows * top), side="right").astype(jnp.int32)
    table = members.reshape(top, rows).T
    table = table[jax.random.permutation(jax.random.fold_in(own, 1), rows)]
    turn = jax.random.randint(jax.random.fold_in(own, 2), (rows, 1), 0, top)
    return jnp.take_along_axis(table, (jnp.arange(top)[None, :] + turn) % top, axis=1)


def shares(number_of, total, reach, skew, full):
    loads = [(1 << 20) // math.isqrt(grade ** skew) + 1 for grade in range(1, number_of + 1)]
    largest = reach if full else min(reach, max(-(-total // number_of), total * loads[0] // sum(loads)))
    least = 1 if total - largest >= number_of - 1 else 0
    holding, surplus = [largest] + [least] * (number_of - 1), total - largest - least * (number_of - 1)
    while surplus > 0:
        movable = [i for i in range(1, number_of) if holding[i] < largest] or [i for i in range(1, number_of) if holding[i] < reach]
        pool, remaining = sum([loads[i] for i in movable]), surplus
        for i in movable:
            addition = min(reach - holding[i], max(1, remaining * loads[i] // pool), surplus)
            holding[i] = holding[i] + addition
            surplus = surplus - addition
    return np.array(holding)


def centred(key, dims, scale, bound, split=(), held_as=jnp.bfloat16):
    values = jax.random.normal(key, dims, jnp.float32) * scale
    if len(split) > 0:
        values = levels(key, dims, split, -0.22, 0.18) * values
    return jnp.clip(values, min=-bound, max=bound).astype(held_as)


def setup_inputs(seed: int = 0) -> dict:
    key_of = jax.random.split(jax.random.key(seed), 11)
    vectors = centred(key_of[0], (NRHS, UNKNOWNS), 1.0, 6.0, ((0, 4), (1, 64)))
    near_field_tiles = centred(key_of[1], (NLEAF, NEAR, LEAF, LEAF), (NEAR * LEAF) ** -0.5, 0.125, ((0, 64), (1, 4)))
    near_lists = draw_near_lists(jax.random.fold_in(key_of[10], 71), 0)
    leaf_basis_set = centred(key_of[3], (NLEAF, RANK, LEAF), LEAF ** -0.5, 0.375, ((0, 64),))
    far_coupling = centred(key_of[4], (NLEAF, RANK, FAR * RANK), RANK ** -0.5, 1.0, ((0, 64),))
    far_device_keys = jax.random.split(jax.random.fold_in(key_of[5], 1), NLEAF // L_DEV)
    far_device_turns = jax.random.permutation(jax.random.fold_in(key_of[5], 3), NLEAF // L_DEV)
    far_device = jax.vmap(lambda own, number: routed_block(jax.random.fold_in(key_of[5], 2), own, number, L_DEV, N_CLUS, FAR, CAP, 2))(far_device_keys, far_device_turns).reshape((NLEAF, FAR))
    far_leaf = place_ends(jax.random.randint(key_of[6], (NLEAF, FAR), 0, L_DEV), jax.random.fold_in(key_of[6], 1), 0, L_DEV - 1).astype(jnp.int32)
    transfer = centred(key_of[7], (NLEAF, RANK, RANK), (RANK * L_DEV) ** -0.5, 0.25, ((0, 64),))
    parent = draw_parent(jax.random.fold_in(key_of[10], 71), 0)
    top_coupling = centred(key_of[9], (NTOP * RANK, NTOP * RANK), (NTOP * RANK) ** -0.5, 0.125, ((0, 64),))
    return dict(vectors=vectors, near_field_tiles=near_field_tiles, near_lists=near_lists, leaf_basis_set=leaf_basis_set, far_coupling=far_coupling, far_device=far_device, far_leaf=far_leaf, transfer=transfer, parent=parent, top_coupling=top_coupling)


def apply_operator(vectors, near_field_tiles, near_lists, leaf_basis_set, far_coupling, far_device, far_leaf, transfer, parent, top_coupling):
    blocked = vectors.astype(jnp.float32).reshape(NRHS, NLEAF, LEAF).transpose(1, 2, 0)
    group_size = math.gcd(NLEAF, 16)

    def near_group(grouped):
        tiles_group, lists_group = grouped
        gathered = blocked[lists_group]
        return jnp.einsum("gpkm,gpmc->gkc", tiles_group.astype(jnp.float32), gathered)

    near_part = lax.map(near_group, (near_field_tiles.reshape(NLEAF // group_size, group_size, NEAR, LEAF, LEAF), near_lists.reshape(NLEAF // group_size, group_size, NEAR)))
    near_part = near_part.reshape(NLEAF, LEAF, NRHS)
    coeffs = jnp.einsum("lrk,lkc->lrc", leaf_basis_set.astype(jnp.float32), blocked)
    coeff32 = lax.optimization_barrier(coeffs.astype(jnp.bfloat16)).astype(jnp.float32)
    contrib = jnp.einsum("lrm,lrc->lmc", far_coupling.astype(jnp.float32), coeff32)
    contrib = lax.optimization_barrier(contrib.astype(jnp.bfloat16)).astype(jnp.float32)
    contrib = contrib.reshape(NLEAF * FAR, RANK, NRHS)
    targets = (far_device * L_DEV + far_leaf).reshape(-1).astype(jnp.int32)
    far_sum = jax.ops.segment_sum(contrib, targets, num_segments=NLEAF)
    upward = jnp.einsum("lrs,lrc->lsc", transfer.astype(jnp.float32), coeff32)
    top_expansion = jax.ops.segment_sum(upward, parent, num_segments=NTOP).astype(jnp.bfloat16)
    top_local = jnp.dot(top_coupling, top_expansion.reshape(NTOP * RANK, NRHS), preferred_element_type=jnp.float32)
    top_local = lax.optimization_barrier(top_local.astype(jnp.bfloat16)).reshape(NTOP, RANK, NRHS)
    chosen = top_local[parent].astype(jnp.float32)
    downward = jnp.einsum("lrs,lsc->lrc", transfer.astype(jnp.float32), chosen)
    local_expansion = lax.optimization_barrier((far_sum + downward).astype(jnp.bfloat16)).astype(jnp.float32)
    far_part = jnp.einsum("lrk,lrc->lkc", leaf_basis_set.astype(jnp.float32), local_expansion)
    joined_result = (near_part + far_part).transpose(2, 0, 1).reshape(NRHS, NLEAF * LEAF)
    return joined_result.astype(jnp.bfloat16)


def reference(vectors, near_field_tiles, near_lists, leaf_basis_set, far_coupling, far_device, far_leaf, transfer, parent, top_coupling):
    first_product = apply_operator(vectors, near_field_tiles, near_lists, leaf_basis_set, far_coupling, far_device, far_leaf, transfer, parent, top_coupling)
    second_product = apply_operator(first_product, near_field_tiles, near_lists, leaf_basis_set, far_coupling, far_device, far_leaf, transfer, parent, top_coupling)
    return (first_product, second_product)
```

```python
import jax
import jax.numpy as jnp
from jax import lax
from jax.sharding import PartitionSpec as P


def extended(block, sides, width):
    for axis, dim in sides:
        count = lax.axis_size(axis)
        forward = [(i, i + 1) for i in range(count - 1)]
        forward.append((count - 1, 0))
        backward = [(target, source) for source, target in forward]
        low = lax.ppermute(
            lax.slice_in_dim(block, block.shape[dim] - width, None, axis=dim), axis, forward
        )
        high = lax.ppermute(lax.slice_in_dim(block, 0, width, axis=dim), axis, backward)
        block = jnp.concatenate([low, block, high], axis=dim)
    return block


def gather_blocks(window, near_lists, leaf_size):
    column_count = window.shape[0]
    leaf_count = near_lists.shape[0]
    every_leaf = leaf_count * lax.axis_size("clus")
    own_leaves = lax.axis_index("clus") * leaf_count + jnp.arange(leaf_count, dtype=jnp.int32)
    offset = (near_lists - own_leaves[:, None] + leaf_count + every_leaf) % every_leaf - leaf_count
    block_index = leaf_count + jnp.arange(leaf_count, dtype=jnp.int32)[:, None] + offset
    reshaped_rows = window.reshape(column_count, 3 * leaf_count, leaf_size)
    return reshaped_rows[:, block_index, :]


def near_terms(window, near_lists, near_field_tiles):
    leaf_size = near_field_tiles.shape[2]
    block_list = gather_blocks(window, near_lists, leaf_size)
    partial_near = jnp.einsum(
        "snea,xsna->xse", near_field_tiles, block_list, preferred_element_type=jnp.float32
    )
    return partial_near.reshape(partial_near.shape[0], -1)


def far_field(
    vectors, leaf_basis_set, far_coupling, far_device, far_leaf, transfer, parent, top_coupling
):
    column_count = vectors.shape[0]
    leaf_count, rank_size, leaf_size = leaf_basis_set.shape
    far_count = far_device.shape[1]
    clusters = lax.axis_size("clus")
    capacity = min(leaf_count, max(2, 2 * leaf_count * far_count // clusters))
    reshaped_rows = vectors.reshape(column_count, leaf_count, leaf_size)
    coeffs = jnp.einsum(
        "jbo,fjo->jbf", leaf_basis_set, reshaped_rows, preferred_element_type=jnp.float32
    ).astype(jnp.bfloat16)
    contrib = jnp.einsum(
        "lrm,lrc->lmc", far_coupling, coeffs, preferred_element_type=jnp.float32
    ).astype(jnp.bfloat16)
    payload = contrib.reshape(leaf_count * far_count, rank_size * column_count)
    destination = far_device.reshape(-1)
    onehot = (destination[:, None] == jnp.arange(clusters, dtype=jnp.int32)[None, :]).astype(
        jnp.int32
    )
    earlier = jnp.cumsum(onehot, axis=0) - onehot
    slot_rank = jnp.sum(earlier * onehot, axis=1)
    position = destination * capacity + slot_rank
    outgoing = (
        jnp.zeros((clusters * capacity, payload.shape[1]), jnp.bfloat16).at[position].set(payload)
    )
    targets = (
        jnp.zeros((clusters * capacity,), jnp.int32).at[position].set(far_leaf.reshape(-1) + 1)
    )
    upward = jnp.einsum(
        "lrs,lrc->lsc", transfer, coeffs, preferred_element_type=jnp.float32
    ).reshape(leaf_count, -1)
    parent_hot = (parent % 2)[:, None] == jnp.arange(2, dtype=jnp.int32)[None, :]
    partial_top = jnp.dot(
        parent_hot.astype(jnp.float32).T,
        upward,
        precision=lax.Precision.HIGHEST,
        preferred_element_type=jnp.float32,
    ).astype(jnp.bfloat16)
    everything = jnp.concatenate(
        [
            outgoing.reshape(clusters, capacity, -1),
            jnp.broadcast_to(partial_top[None], (clusters,) + partial_top.shape),
        ],
        axis=1,
    )
    arrived = lax.all_to_all(everything, "clus", split_axis=0, concat_axis=0, tiled=True)
    arrived_ids = lax.all_to_all(
        targets.reshape(clusters, capacity), "clus", split_axis=0, concat_axis=0, tiled=True
    )
    picker = (
        arrived_ids.reshape(1, -1) == jnp.arange(1, leaf_count + 1, dtype=jnp.int32)[:, None]
    ).astype(jnp.bfloat16)
    far_sum = jnp.dot(
        picker,
        arrived[:, :capacity].reshape(clusters * capacity, -1),
        preferred_element_type=jnp.float32,
    )
    top_pairs = arrived[:, capacity:].astype(jnp.float32)
    top_pairs = top_pairs.reshape(clusters // 2, 2, 2, -1).sum(axis=1).astype(jnp.bfloat16)
    top_expansion = jnp.roll(top_pairs.reshape(clusters, -1), clusters // 2, axis=0)
    own_top = jnp.dot(
        top_coupling,
        top_expansion.reshape(clusters * rank_size, column_count),
        preferred_element_type=jnp.float32,
    ).astype(jnp.bfloat16)
    chosen = jnp.dot(
        parent_hot.astype(jnp.bfloat16),
        own_top.reshape(2, -1),
        preferred_element_type=jnp.float32,
    )
    chosen = chosen.astype(jnp.bfloat16).reshape(leaf_count, rank_size, column_count)
    downward = jnp.einsum("lrs,lsc->lrc", transfer, chosen, preferred_element_type=jnp.float32)
    local_expansion = (far_sum.reshape(leaf_count, rank_size, column_count) + downward).astype(
        jnp.bfloat16
    )
    far_out = jnp.einsum(
        "aex,aeu->uax", leaf_basis_set, local_expansion, preferred_element_type=jnp.float32
    )
    return far_out.reshape(column_count, -1)


def on_device(
    vectors,
    near_field_tiles,
    near_lists,
    leaf_basis_set,
    far_coupling,
    far_device,
    far_leaf,
    transfer,
    parent,
    top_coupling,
):
    clusters = lax.axis_size("clus")
    across = lax.ppermute(
        top_coupling, "clus", [(i, (i + clusters // 2) % clusters) for i in range(clusters)]
    )
    other = lax.ppermute(across, "clus", [(i, i ^ 1) for i in range(clusters)])
    core = lax.axis_index("clus") % 2
    top_coupling = jnp.where(
        core == 0,
        jnp.concatenate([across, other], axis=0),
        jnp.concatenate([other, across], axis=0),
    )
    current = vectors
    results = []
    for repeat in range(2):
        halo_width = current.shape[1]
        everyone = lax.all_gather(current, "rhs", axis=0, tiled=True)
        window = extended(everyone, (("clus", 1),), halo_width)
        near_sum = lax.psum_scatter(
            near_terms(window, near_lists, near_field_tiles), "rhs", scatter_dimension=0, tiled=True
        )
        far_sum = far_field(
            current,
            leaf_basis_set,
            far_coupling,
            far_device,
            far_leaf,
            transfer,
            parent,
            top_coupling,
        )
        current = (near_sum + far_sum).astype(jnp.bfloat16)
        results.append(current)
    return (results[0], results[1])


def solution(mesh):
    placed = (
        P("rhs", "clus"),
        P("clus", "rhs", None, None),
        P("clus", "rhs"),
        P("clus", None, None),
        P("clus", None, None),
        P("clus", None),
        P("clus", None),
        P("clus", None, None),
        P("clus"),
        P("clus", None),
    )
    return jax.shard_map(
        on_device,
        mesh=mesh,
        in_specs=placed,
        out_specs=(P("rhs", "clus"), P("rhs", "clus")),
        check_vma=False,
    )
```

```python
import jax
import jax.numpy as jnp
from jax import lax
from jax.experimental import pallas as pl
from jax.experimental.pallas import tpu as pltpu
from jax.sharding import PartitionSpec as P

MESH = pl.DeviceIdType.MESH
BF16 = jnp.bfloat16
F32 = jnp.float32
CLUS, RHS = 64, 4
LEAVES, RANK, LEAF, COLS = 16, 32, 256, 16
FAR, SLOTS, GROUPS = 8, 4, 4
LANES = 128
EMPTY = LEAVES * FAR


def dot_nn(a, b):
    return lax.dot_general(a, b, (((1,), (0,)), ((), ())), preferred_element_type=F32)


def dot_nt(a, b):
    return lax.dot_general(a, b, (((1,), (1,)), ((), ())), preferred_element_type=F32)


def kernel(
    near_s, source_s,
    vec_h, tiles_h, basis_h, coup_h, tr_h, topc_h, ids_h,
    out1, out2,
    vec, tiles, basis, coup, tr, topc, ids_in,
    win0, win1, part, rs, rolled, far,
    term_out, term_in, pair_out, pair_in, top_out, top_in, down_out, down_in,
    load_sem, ag_s, ag_r, halo_s, halo_r, rs_s, rs_r,
    term_s, term_r, id_s, id_r, pair_s, pair_r, top_s, top_r, down_s, down_r,
):
    me = lax.axis_index("clus")
    row = lax.axis_index("rhs")
    sibling = me + 1 - 2 * lax.rem(me, 2)
    above = lax.rem(me + 1, CLUS)
    below = lax.rem(me + CLUS - 1, CLUS)

    def send(src, dst, s, r, device):
        return pltpu.make_async_remote_copy(
            src_ref=src, dst_ref=dst, send_sem=s, recv_sem=r, device_id=device, device_id_type=MESH
        )

    barrier = pltpu.get_barrier_semaphore()

    def greet(o, c):
        pl.semaphore_signal(
            barrier, inc=1, device_id=(lax.rem(me + o, CLUS), row), device_id_type=MESH
        )
        return c

    lax.fori_loop(1, CLUS, greet, 0)
    for o in range(1, RHS):
        pl.semaphore_signal(
            barrier, inc=1, device_id=(me, lax.rem(row + o, RHS)), device_id_type=MESH
        )

    loads = [
        pltpu.make_async_copy(vec_h, vec, load_sem.at[0]),
        pltpu.make_async_copy(basis_h, basis, load_sem.at[1]),
        pltpu.make_async_copy(tr_h, tr, load_sem.at[2]),
        pltpu.make_async_copy(coup_h, coup, load_sem.at[3]),
    ]
    for k in range(4):
        loads.append(
            pltpu.make_async_copy(topc_h, topc.at[pl.ds(k * RANK, RANK)], load_sem.at[4 + k])
        )
    loads.append(pltpu.make_async_copy(tiles_h, tiles, load_sem.at[8]))
    for copy in loads:
        copy.start()
    rolled[EMPTY] = jnp.zeros((COLS, LANES), F32)

    lane = lax.broadcasted_iota(jnp.int32, (COLS, LANES), 1) // RANK
    group_row = lax.broadcasted_iota(jnp.int32, (GROUPS * COLS, LANES), 0) // COLS
    group_lane = lax.broadcasted_iota(jnp.int32, (GROUPS * COLS, LANES), 1) // RANK
    diagonal = group_row == group_lane
    zero = jnp.zeros((COLS, LANES), F32)

    loads[0].wait()
    for i in range(LEAVES):
        win0[row, LEAVES + i] = vec[:, i * LEAF : (i + 1) * LEAF]
    loads[1].wait()
    loads[2].wait()

    pending = []
    for q in range(2):
        win = (win0, win1)[q]
        own = win.at[row, pl.ds(LEAVES, LEAVES)]

        def spread(o, source):
            block = win.at[source, pl.ds(LEAVES, LEAVES)]
            up = send(block, win.at[source, pl.ds(0, LEAVES)],
                      halo_s.at[q, 0, o], halo_r.at[q, 0, o], (above, row))
            dn = send(block, win.at[source, pl.ds(2 * LEAVES, LEAVES)],
                      halo_s.at[q, 1, o], halo_r.at[q, 1, o], (below, row))
            return [up, dn]

        if q == 0:
            pl.semaphore_wait(barrier, CLUS - 1 + RHS - 1)
        gathers = [
            send(own, own, ag_s.at[q, o - 1], ag_r.at[q, o - 1], (me, lax.rem(row + o, RHS)))
            for o in range(1, RHS)
        ]
        halos = spread(0, row)
        for copy in (gathers[0], gathers[2], gathers[1], halos[0], halos[1]):
            copy.start()

        coeffs = []
        top_sum = zero
        for g in range(GROUPS):
            values = win[row, LEAVES + GROUPS * g : LEAVES + GROUPS * (g + 1)]
            values = values.reshape(GROUPS * COLS, LEAF)
            product = dot_nt(values, basis[g * LANES : (g + 1) * LANES, :])
            product = jnp.where(diagonal, product, 0.0)
            masked = product.astype(BF16)
            coeffs.append(masked)
            joined = product[0:COLS]
            for t in range(1, GROUPS):
                joined = joined + product[t * COLS : (t + 1) * COLS]
            top_sum = top_sum + dot_nn(joined.astype(BF16), tr[g * LANES : (g + 1) * LANES, :])
        pair_out[q] = top_sum
        pair = send(pair_out.at[q], pair_in.at[q], pair_s.at[q], pair_r.at[q], (sibling, row))
        pair.start()
        pending.append(pair)

        if q == 0:
            loads[3].wait()
        for g in range(GROUPS):
            terms = dot_nn(coeffs[g], coup[g * LANES : (g + 1) * LANES, :])
            for t in range(GROUPS):
                for half in range(2):
                    tile = terms[t * COLS : (t + 1) * COLS, half * LANES : (half + 1) * LANES]
                    base = (GROUPS * g + t) * FAR + half * 4
                    rolled[base] = tile
                    for k in range(1, 4):
                        rolled[base + k] = pltpu.roll(tile, RANK * k, 1)

        pair.wait_recv()
        top_tile = (top_sum + pair_in[q]).astype(BF16)
        top_out[q] = top_tile
        top_in[q, me // 2] = top_tile

        def top_copy(o):
            return send(top_out.at[q], top_in.at[q, me // 2], top_s.at[q], top_r.at[q],
                        (lax.rem(me + 2 * o, CLUS), row))

        def top_start(o, c):
            top_copy(o).start()
            return c

        lax.fori_loop(1, CLUS // 2, top_start, 0)

        def packed(d):
            parts = [rolled[source_s[d * SLOTS + s]] for s in range(SLOTS)]
            low = jnp.where(lane == 0, parts[0], parts[1])
            high = jnp.where(lane == 2, parts[2], parts[3])
            return jnp.where(lane < 2, low, high).astype(BF16)

        def term_copy(d):
            return send(term_out.at[q, d], term_in.at[q, me], term_s.at[q], term_r.at[q], (d, row))

        def id_copy(d):
            return send(ids_h.at[d], ids_in.at[me], id_s, id_r, (d, row))

        def term_start(o, c):
            d = lax.rem(me + o, CLUS)
            term_out[q, d] = packed(d)
            term_copy(d).start()
            if q == 0:
                id_copy(d).start()
            return c

        lax.fori_loop(1, CLUS, term_start, 0)
        term_in[q, me] = packed(me)
        if q == 0:
            own_ids = pltpu.make_async_copy(ids_h.at[me], ids_in.at[me], load_sem.at[9])
            own_ids.start()

        for o in (1, 3, 2):
            gathers[o - 1].wait_recv()
            more = spread(o, lax.rem(row + RHS - o, RHS))
            for copy in more:
                copy.start()
            halos += more
        pending += gathers + halos

        if q == 0:
            for k in range(4):
                loads[4 + k].wait()
        pltpu.make_async_copy(
            top_in.at[q, pl.ds(0, CLUS // 2 - 1)], top_in.at[q, pl.ds(0, CLUS // 2 - 1)], top_r.at[q]
        ).wait()
        pairs = CLUS // 4
        tops = [None] * pairs
        for m in range(pairs):
            tops[(m + pairs // 2) % pairs] = top_in[q, 2 * m] + top_in[q, 2 * m + 1]
        local = dot_nt(jnp.concatenate(tops, axis=1), topc[...])
        down_out[q] = jnp.where(lane == lax.rem(me, 4), local, 0.0).astype(BF16)
        across = lax.rem(me + CLUS // 2, CLUS)
        for k, d in enumerate((across, across + 1 - 2 * lax.rem(across, 2))):
            copy = send(down_out.at[q], down_in.at[q, k],
                        down_s.at[q, k], down_r.at[q, k], (d, row))
            copy.start()
            pending.append(copy)
        downs = pending[-2:]

        for copy in halos:
            copy.wait_recv()
        if q == 0:
            loads[8].wait()

        def rs_copy(chunk, o):
            leaves = pl.ds(chunk * GROUPS, GROUPS)
            target = lax.rem(row + o, RHS)
            return send(part.at[q, target, leaves], rs.at[q, o - 1, leaves],
                        rs_s.at[q, o - 1, chunk], rs_r.at[q, o - 1, chunk], (me, target))

        def near_chunk(chunk, c):
            for n in range(GROUPS):
                leaf = chunk * GROUPS + n
                total = None
                for p in range(2):
                    j = near_s[leaf * 2 + p]
                    slot = lax.rem(j - me * LEAVES + LEAVES + CLUS * LEAVES, CLUS * LEAVES)
                    slot = jnp.minimum(slot, 3 * LEAVES - 1)
                    block = win[:, slot].reshape(RHS * COLS, LEAF)
                    product = dot_nt(block, tiles[leaf, p])
                    total = product if total is None else total + product
                for a in range(RHS):
                    part[q, a, leaf] = total[a * COLS : (a + 1) * COLS].astype(BF16)
            for o in (2, 1, 3):
                rs_copy(chunk, o).start()
            return c

        lax.fori_loop(0, GROUPS, near_chunk, 0)

        pltpu.make_async_copy(
            term_in.at[q, pl.ds(0, CLUS - 1)], term_in.at[q, pl.ds(0, CLUS - 1)], term_r.at[q]
        ).wait()
        if q == 0:
            own_ids.wait()
            pltpu.make_async_copy(
                ids_in.at[pl.ds(0, CLUS - 1)], ids_in.at[pl.ds(0, CLUS - 1)], id_r
            ).wait()

        def add_terms(s, sums):
            values = term_in[q, s].astype(F32)
            targets = ids_in[s].astype(F32)
            return tuple(
                sums[t] + jnp.where(targets == float(t + 1), values, 0.0) for t in range(LEAVES)
            )

        sums = lax.fori_loop(0, CLUS, add_terms, (zero,) * LEAVES)

        for copy in downs:
            copy.wait_recv()
        chosen = down_in[q, 0] + down_in[q, 1]
        for g in range(GROUPS):
            down = dot_nt(chosen, tr[g * LANES : (g + 1) * LANES, :])
            rows = []
            for t in range(GROUPS):
                x = sums[GROUPS * g + t]
                x = x + pltpu.roll(x, 2 * RANK, 1)
                x = x + pltpu.roll(x, RANK, 1)
                rows.append(jnp.where(lane == t, x + down, 0.0).astype(BF16))
            result = dot_nn(jnp.concatenate(rows, axis=0), basis[g * LANES : (g + 1) * LANES, :])
            for t in range(GROUPS):
                far[GROUPS * g + t] = result[t * COLS : (t + 1) * COLS]

        out = out1 if q == 0 else out2
        for chunk in range(GROUPS):
            for o in range(1, RHS):
                rs_copy(chunk, o).wait_recv()
            for n in range(GROUPS):
                leaf = chunk * GROUPS + n
                total = far[leaf] + part[q, row, leaf].astype(F32)
                for o in range(RHS - 1):
                    total = total + rs[q, o, leaf].astype(F32)
                value = total.astype(BF16)
                out[:, leaf * LEAF : (leaf + 1) * LEAF] = value
                if q == 0:
                    win1[row, LEAVES + leaf] = value
        for chunk in range(GROUPS):
            for o in range(1, RHS):
                pending.append(rs_copy(chunk, o))

    for copy in pending:
        copy.wait_send()
    for q in range(2):
        pltpu.make_async_copy(
            top_in.at[q, pl.ds(0, CLUS // 2 - 1)], top_in.at[q, pl.ds(0, CLUS // 2 - 1)], top_s.at[q]
        ).wait()
        pltpu.make_async_copy(
            term_in.at[q, pl.ds(0, CLUS - 1)], term_in.at[q, pl.ds(0, CLUS - 1)], term_s.at[q]
        ).wait()
    pltpu.make_async_copy(
        ids_in.at[pl.ds(0, CLUS - 1)], ids_in.at[pl.ds(0, CLUS - 1)], id_s
    ).wait()


def slot_tables(far_device, far_leaf):
    target = far_device.reshape(-1)
    count = target.shape[0]
    order = jnp.arange(count, dtype=jnp.int32)
    same = target[:, None] == target[None, :]
    rank = jnp.sum((same & (order[None, :] < order[:, None])).astype(jnp.int32), axis=1)
    partner = order % FAR
    code = (order // FAR) * FAR + (partner // 4) * 4 + (rank - partner + FAR) % 4
    slot = target * SLOTS + rank
    hit = slot[None, :] == jnp.arange(CLUS * SLOTS, dtype=jnp.int32)[:, None]
    source = EMPTY + jnp.sum(jnp.where(hit, code[None, :] - EMPTY, 0), axis=1)
    leaf = jnp.sum(jnp.where(hit, far_leaf.reshape(-1)[None, :] + 1, 0), axis=1)
    tile = jnp.broadcast_to(
        leaf.astype(BF16).reshape(CLUS, 1, SLOTS, 1), (CLUS, COLS, SLOTS, RANK)
    ).reshape(CLUS, COLS, LANES)
    return source.astype(jnp.int32), tile


def on_device(
    vectors, near_field_tiles, near_lists, leaf_basis_set, far_coupling,
    far_device, far_leaf, transfer, parent, top_coupling,
):
    source, ids = slot_tables(far_device, far_leaf)
    chip = lax.axis_index("clus") // 2
    place = (chip % 2) * 2 + parent % 2
    hot = place[:, None, None, None] == jnp.arange(4, dtype=jnp.int32)[None, None, :, None]
    tr = jnp.where(hot, transfer[:, :, None, :], jnp.zeros((), BF16)).reshape(
        LEAVES * RANK, LANES
    )
    vmem = lambda shape, dtype=BF16: pltpu.VMEM(shape, dtype)
    dma = lambda *shape: pltpu.SemaphoreType.DMA(shape)
    anywhere = pl.BlockSpec(memory_space=pl.ANY)
    smem = pl.BlockSpec(memory_space=pltpu.SMEM)
    whole = pl.BlockSpec(memory_space=pltpu.VMEM)
    return pl.pallas_call(
        kernel,
        out_shape=[jax.ShapeDtypeStruct(vectors.shape, BF16)] * 2,
        in_specs=[smem, smem] + [anywhere] * 7,
        out_specs=[whole] * 2,
        scratch_shapes=[
            vmem((COLS, LEAVES * LEAF)),
            vmem((LEAVES, 2, LEAF, LEAF)),
            vmem((LEAVES * RANK, LEAF)),
            vmem((LEAVES * RANK, FAR * RANK)),
            vmem((LEAVES * RANK, LANES)),
            vmem((4 * RANK, CLUS * RANK)),
            vmem((CLUS, COLS, LANES)),
            vmem((RHS, 3 * LEAVES, COLS, LEAF)),
            vmem((RHS, 3 * LEAVES, COLS, LEAF)),
            vmem((2, RHS, LEAVES, COLS, LEAF)),
            vmem((2, RHS - 1, LEAVES, COLS, LEAF)),
            vmem((EMPTY + 1, COLS, LANES), F32),
            vmem((LEAVES, COLS, LEAF), F32),
            vmem((2, CLUS, COLS, LANES)),
            vmem((2, CLUS, COLS, LANES)),
            vmem((2, COLS, LANES), F32),
            vmem((2, COLS, LANES), F32),
            vmem((2, COLS, LANES)),
            vmem((2, CLUS // 2, COLS, LANES)),
            vmem((2, COLS, LANES)),
            vmem((2, 2, COLS, LANES)),
            dma(10),
            dma(2, RHS - 1), dma(2, RHS - 1),
            dma(2, 2, RHS), dma(2, 2, RHS),
            dma(2, RHS - 1, GROUPS), dma(2, RHS - 1, GROUPS),
            dma(2), dma(2),
            pltpu.SemaphoreType.DMA, pltpu.SemaphoreType.DMA,
            dma(2), dma(2),
            dma(2), dma(2),
            dma(2, 2), dma(2, 2),
        ],
        compiler_params=pltpu.CompilerParams(
            collective_id=0, has_side_effects=True, vmem_limit_bytes=40 * 1024 * 1024
        ),
    )(
        near_lists.reshape(-1), source,
        vectors, near_field_tiles,
        leaf_basis_set.reshape(LEAVES * RANK, LEAF),
        far_coupling.reshape(LEAVES * RANK, FAR * RANK),
        tr, top_coupling, ids,
    )


def solution(mesh):
    placed = (
        P("rhs", "clus"),
        P("clus", "rhs", None, None),
        P("clus", "rhs"),
        P("clus", None, None),
        P("clus", None, None),
        P("clus", None),
        P("clus", None),
        P("clus", None, None),
        P("clus"),
        P("clus", None),
    )
    return jax.shard_map(
        on_device,
        mesh=mesh,
        in_specs=placed,
        out_specs=(P("rhs", "clus"), P("rhs", "clus")),
        check_vma=False,
    )
```

```python
import jax
import jax.numpy as jnp
from jax import lax
from jax.experimental import pallas as pl
from jax.experimental.pallas import tpu as pltpu
from jax.sharding import PartitionSpec as P

MESH = pl.DeviceIdType.MESH
BF16 = jnp.bfloat16
F32 = jnp.float32
CLUS, RHS = 64, 4
LEAVES, RANK, LEAF, COLS = 16, 32, 256, 16
FAR, SLOTS, GROUPS = 8, 4, 4
ORDER = (0, 2, 1, 3)
LANES = 128
EMPTY = LEAVES * FAR


def dot_nn(a, b):
    return lax.dot_general(a, b, (((1,), (0,)), ((), ())), preferred_element_type=F32)


def dot_nt(a, b):
    return lax.dot_general(a, b, (((1,), (1,)), ((), ())), preferred_element_type=F32)


def kernel(
    near_s, source_s,
    vec_h, tiles_h, basis_h, coup_h, tr_h, topc_h, ids_h,
    out1, out2,
    vec, tiles, basis, coup, tr, topc, ids_in,
    win0, win1, part, rs, relay, rolled, far,
    term_out, term_in, quad_out, quad_in, top_out, top_in, down_out, down_in,
    load_sem, ag_s, ag_r, halo_s, halo_r, rs_s, rs_r, relay_s, relay_r,
    term_s, term_r, id_s, id_r, quad_s, quad_r, top_s, top_r, down_s, down_r,
):
    me = lax.axis_index("clus")
    row = lax.axis_index("rhs")
    right = lax.rem(row + 1, RHS)
    left = lax.rem(row + RHS - 1, RHS)
    opposite = lax.rem(row + 2, RHS)
    corner = lax.rem(me, 4)
    above = lax.rem(me + 1, CLUS)
    below = lax.rem(me + CLUS - 1, CLUS)

    def send(src, dst, s, r, device):
        return pltpu.make_async_remote_copy(
            src_ref=src, dst_ref=dst, send_sem=s, recv_sem=r, device_id=device, device_id_type=MESH
        )

    barrier = pltpu.get_barrier_semaphore()

    def greet(o, c):
        pl.semaphore_signal(
            barrier, inc=1, device_id=(lax.rem(me + o, CLUS), row), device_id_type=MESH
        )
        return c

    lax.fori_loop(1, CLUS, greet, 0)
    for o in range(1, RHS):
        pl.semaphore_signal(
            barrier, inc=1, device_id=(me, lax.rem(row + o, RHS)), device_id_type=MESH
        )

    loads = [
        pltpu.make_async_copy(vec_h, vec, load_sem.at[0]),
        pltpu.make_async_copy(basis_h, basis, load_sem.at[1]),
        pltpu.make_async_copy(tr_h, tr, load_sem.at[2]),
        pltpu.make_async_copy(coup_h, coup, load_sem.at[3]),
    ]
    for k in range(4):
        loads.append(
            pltpu.make_async_copy(topc_h, topc.at[pl.ds(k * RANK, RANK)], load_sem.at[4 + k])
        )
    loads.append(pltpu.make_async_copy(tiles_h, tiles, load_sem.at[8]))
    for copy in loads:
        copy.start()
    rolled[EMPTY] = jnp.zeros((COLS, LANES), F32)

    lane = lax.broadcasted_iota(jnp.int32, (COLS, LANES), 1) // RANK
    group_row = lax.broadcasted_iota(jnp.int32, (GROUPS * COLS, LANES), 0) // COLS
    group_lane = lax.broadcasted_iota(jnp.int32, (GROUPS * COLS, LANES), 1) // RANK
    diagonal = group_row == group_lane
    zero = jnp.zeros((COLS, LANES), F32)

    loads[0].wait()
    for i in range(LEAVES):
        win0[row, LEAVES + i] = vec[:, i * LEAF : (i + 1) * LEAF]
    loads[1].wait()
    loads[2].wait()

    pending = []

    def own_chunk(q, chunk):
        win = (win0, win1)[q]
        block = win.at[row, pl.ds(LEAVES + GROUPS * chunk, GROUPS)]
        copies = [
            send(block, block, ag_s.at[q, 0, chunk], ag_r.at[q, 0, chunk], (me, right)),
            send(block, block, ag_s.at[q, 1, chunk], ag_r.at[q, 1, chunk], (me, left)),
        ] + spread(q, 0, row, chunk)
        for copy in copies:
            copy.start()
        pending.extend(copies)

    def spread(q, o, source, chunk):
        win = (win0, win1)[q]
        base = GROUPS * chunk
        block = win.at[source, pl.ds(LEAVES + base, GROUPS)]
        return [
            send(block, win.at[source, pl.ds(base, GROUPS)],
                 halo_s.at[q, 0, o, chunk], halo_r.at[q, 0, o, chunk], (above, row)),
            send(block, win.at[source, pl.ds(2 * LEAVES + base, GROUPS)],
                 halo_s.at[q, 1, o, chunk], halo_r.at[q, 1, o, chunk], (below, row)),
        ]

    for q in range(2):
        win = (win0, win1)[q]
        if q == 0:
            pl.semaphore_wait(barrier, CLUS - 1 + RHS - 1)
            for chunk in ORDER:
                own_chunk(0, chunk)

        coeffs = []
        top_sum = zero
        for g in range(GROUPS):
            values = win[row, LEAVES + GROUPS * g : LEAVES + GROUPS * (g + 1)]
            values = values.reshape(GROUPS * COLS, LEAF)
            product = dot_nt(values, basis[g * LANES : (g + 1) * LANES, :])
            product = jnp.where(diagonal, product, 0.0)
            masked = product.astype(BF16)
            coeffs.append(masked)
            joined = product[0:COLS]
            for t in range(1, GROUPS):
                joined = joined + product[t * COLS : (t + 1) * COLS]
            top_sum = top_sum + dot_nn(joined.astype(BF16), tr[g * LANES : (g + 1) * LANES, :])
        quad_out[q] = top_sum
        quads = []
        for o in range(1, 4):
            peer = me - corner + lax.rem(corner + o, 4)
            copy = send(quad_out.at[q], quad_in.at[q, o - 1],
                        quad_s.at[q, o - 1], quad_r.at[q, o - 1], (peer, row))
            copy.start()
            quads.append(copy)
        pending += quads

        if q == 0:
            loads[3].wait()
        for g in range(GROUPS):
            terms = dot_nn(coeffs[g], coup[g * LANES : (g + 1) * LANES, :])
            for t in range(GROUPS):
                for half in range(2):
                    tile = terms[t * COLS : (t + 1) * COLS, half * LANES : (half + 1) * LANES]
                    base = (GROUPS * g + t) * FAR + half * 4
                    rolled[base] = tile
                    for k in range(1, 4):
                        rolled[base + k] = pltpu.roll(tile, RANK * k, 1)

        for copy in quads:
            copy.wait_recv()
        top_tile = (top_sum + quad_in[q, 0] + quad_in[q, 1] + quad_in[q, 2]).astype(BF16)
        top_out[q] = top_tile
        top_in[q, me // 4] = top_tile

        def top_start(o, c):
            send(top_out.at[q], top_in.at[q, me // 4], top_s.at[q], top_r.at[q],
                 (lax.rem(me + 4 * o, CLUS), row)).start()
            return c

        lax.fori_loop(1, CLUS // 4, top_start, 0)

        def packed(d):
            parts = [rolled[source_s[d * SLOTS + s]] for s in range(SLOTS)]
            low = jnp.where(lane == 0, parts[0], parts[1])
            high = jnp.where(lane == 2, parts[2], parts[3])
            return jnp.where(lane < 2, low, high).astype(BF16)

        def term_copy(d):
            return send(term_out.at[q, d], term_in.at[q, me], term_s.at[q], term_r.at[q], (d, row))

        def id_copy(d):
            return send(ids_h.at[d], ids_in.at[me], id_s, id_r, (d, row))

        def term_start(o, c):
            d = lax.rem(me + o, CLUS)
            term_out[q, d] = packed(d)
            term_copy(d).start()
            if q == 0:
                id_copy(d).start()
            return c

        lax.fori_loop(1, CLUS, term_start, 0)
        term_in[q, me] = packed(me)
        if q == 0:
            own_ids = pltpu.make_async_copy(ids_h.at[me], ids_in.at[me], load_sem.at[9])
            own_ids.start()

        halos = []
        for chunk in ORDER:
            for side, source in enumerate((left, right)):
                block = win.at[source, pl.ds(LEAVES + GROUPS * chunk, GROUPS)]
                send(block, block, ag_s.at[q, side, chunk], ag_r.at[q, side, chunk],
                     (me, right)).wait_recv()
                more = spread(q, 1 + 2 * side, source, chunk)
                if side == chunk // 2:
                    more.insert(0, send(block, block, ag_s.at[q, 2, chunk], ag_r.at[q, 2, chunk],
                                        (me, (right, left)[side])))
                for copy in more:
                    copy.start()
                pending += more
        for chunk in ORDER:
            block = win.at[opposite, pl.ds(LEAVES + GROUPS * chunk, GROUPS)]
            send(block, block, ag_s.at[q, 2, chunk], ag_r.at[q, 2, chunk], (me, right)).wait_recv()
            more = spread(q, 2, opposite, chunk)
            for copy in more:
                copy.start()
            pending += more

        if q == 0:
            for k in range(4):
                loads[4 + k].wait()
        pltpu.make_async_copy(
            top_in.at[q, pl.ds(0, CLUS // 4 - 1)], top_in.at[q, pl.ds(0, CLUS // 4 - 1)], top_r.at[q]
        ).wait()
        pairs = CLUS // 4
        tops = [None] * pairs
        for m in range(pairs):
            tops[(m + pairs // 2) % pairs] = top_in[q, m]
        local = dot_nt(jnp.concatenate(tops, axis=1), topc[...])
        down_out[q] = jnp.where(lane == lax.rem(me, 4), local, 0.0).astype(BF16)
        across = lax.rem(me + CLUS // 2, CLUS)
        for k, d in enumerate((across, across + 1 - 2 * lax.rem(across, 2))):
            copy = send(down_out.at[q], down_in.at[q, k],
                        down_s.at[q, k], down_r.at[q, k], (d, row))
            copy.start()
            pending.append(copy)
        downs = pending[-2:]

        for chunk in ORDER:
            for o, source in ((0, row), (1, left), (3, right), (2, opposite)):
                for copy in spread(q, o, source, chunk):
                    copy.wait_recv()
        if q == 0:
            loads[8].wait()

        def relay_copy(chunk):
            leaves = pl.ds(chunk * GROUPS, GROUPS)
            return send(part.at[q, opposite, leaves], relay.at[q, leaves],
                        relay_s.at[q, chunk], relay_r.at[q, chunk],
                        (me, (right, left)[chunk // 2]))

        def rs_copy(chunk, side):
            leaves = pl.ds(chunk * GROUPS, GROUPS)
            target = (right, left)[side]
            return send(part.at[q, target, leaves], rs.at[q, side, leaves],
                        rs_s.at[q, side, chunk], rs_r.at[q, side, chunk], (me, target))

        def near_chunk(chunk):
            for n in range(GROUPS):
                leaf = chunk * GROUPS + n
                total = None
                for p in range(2):
                    j = near_s[leaf, p]
                    slot = lax.rem(j - me * LEAVES + LEAVES + CLUS * LEAVES, CLUS * LEAVES)
                    slot = jnp.minimum(slot, 3 * LEAVES - 1)
                    block = win[:, slot].reshape(RHS * COLS, LEAF)
                    product = dot_nt(block, tiles[leaf, p])
                    total = product if total is None else total + product
                for a in range(RHS):
                    part[q, a, leaf] = total[a * COLS : (a + 1) * COLS].astype(BF16)
            copies = (relay_copy(chunk), rs_copy(chunk, 1 - chunk // 2))
            for copy in copies:
                copy.start()
            pending.extend(copies)

        for chunk in ORDER:
            near_chunk(chunk)
        for chunk in ORDER:
            relay_copy(chunk).wait_recv()
            side = chunk // 2
            target = (right, left)[side]
            for n in range(GROUPS):
                leaf = chunk * GROUPS + n
                part[q, target, leaf] = (
                    part[q, target, leaf].astype(F32) + relay[q, leaf].astype(F32)
                ).astype(BF16)
            copy = rs_copy(chunk, side)
            copy.start()
            pending.append(copy)

        pltpu.make_async_copy(
            term_in.at[q, pl.ds(0, CLUS - 1)], term_in.at[q, pl.ds(0, CLUS - 1)], term_r.at[q]
        ).wait()
        if q == 0:
            own_ids.wait()
            pltpu.make_async_copy(
                ids_in.at[pl.ds(0, CLUS - 1)], ids_in.at[pl.ds(0, CLUS - 1)], id_r
            ).wait()

        def add_terms(s, sums):
            values = term_in[q, s].astype(F32)
            targets = ids_in[s].astype(F32)
            return tuple(
                sums[t] + jnp.where(targets == float(t + 1), values, 0.0) for t in range(LEAVES)
            )

        sums = lax.fori_loop(0, CLUS, add_terms, (zero,) * LEAVES)

        for copy in downs:
            copy.wait_recv()
        chosen = down_in[q, 0] + down_in[q, 1]
        for g in range(GROUPS):
            down = dot_nt(chosen, tr[g * LANES : (g + 1) * LANES, :])
            rows = []
            for t in range(GROUPS):
                x = sums[GROUPS * g + t]
                x = x + pltpu.roll(x, 2 * RANK, 1)
                x = x + pltpu.roll(x, RANK, 1)
                rows.append(jnp.where(lane == t, x + down, 0.0).astype(BF16))
            result = dot_nn(jnp.concatenate(rows, axis=0), basis[g * LANES : (g + 1) * LANES, :])
            for t in range(GROUPS):
                far[GROUPS * g + t] = result[t * COLS : (t + 1) * COLS]

        out = out1 if q == 0 else out2
        for chunk in ORDER:
            rs_copy(chunk, 1 - chunk // 2).wait_recv()
            rs_copy(chunk, chunk // 2).wait_recv()
            for n in range(GROUPS):
                leaf = chunk * GROUPS + n
                total = far[leaf] + part[q, row, leaf].astype(F32)
                total = total + rs[q, 0, leaf].astype(F32) + rs[q, 1, leaf].astype(F32)
                value = total.astype(BF16)
                out[:, leaf * LEAF : (leaf + 1) * LEAF] = value
                if q == 0:
                    win1[row, LEAVES + leaf] = value
            if q == 0:
                own_chunk(1, chunk)

    for copy in pending:
        copy.wait_send()
    for q in range(2):
        pltpu.make_async_copy(
            top_in.at[q, pl.ds(0, CLUS // 4 - 1)], top_in.at[q, pl.ds(0, CLUS // 4 - 1)], top_s.at[q]
        ).wait()
        pltpu.make_async_copy(
            term_in.at[q, pl.ds(0, CLUS - 1)], term_in.at[q, pl.ds(0, CLUS - 1)], term_s.at[q]
        ).wait()
    pltpu.make_async_copy(
        ids_in.at[pl.ds(0, CLUS - 1)], ids_in.at[pl.ds(0, CLUS - 1)], id_s
    ).wait()


def slot_tables(far_device, far_leaf):
    target = far_device.reshape(-1)
    count = target.shape[0]
    order = jnp.arange(count, dtype=jnp.int32)
    same = target[:, None] == target[None, :]
    rank = jnp.sum((same & (order[None, :] < order[:, None])).astype(jnp.int32), axis=1)
    partner = order % FAR
    code = (order // FAR) * FAR + (partner // 4) * 4 + (rank - partner + FAR) % 4
    slot = target * SLOTS + rank
    hit = slot[None, :] == jnp.arange(CLUS * SLOTS, dtype=jnp.int32)[:, None]
    source = EMPTY + jnp.sum(jnp.where(hit, code[None, :] - EMPTY, 0), axis=1)
    leaf = jnp.sum(jnp.where(hit, far_leaf.reshape(-1)[None, :] + 1, 0), axis=1)
    tile = jnp.broadcast_to(
        leaf.astype(BF16).reshape(CLUS, 1, SLOTS, 1), (CLUS, COLS, SLOTS, RANK)
    ).reshape(CLUS, COLS, LANES)
    return source.astype(jnp.int32), tile


def on_device(
    vectors, near_field_tiles, near_lists, leaf_basis_set, far_coupling,
    far_device, far_leaf, transfer, parent, top_coupling,
):
    source, ids = slot_tables(far_device, far_leaf)
    chip = lax.axis_index("clus") // 2
    place = (chip % 2) * 2 + parent % 2
    hot = place[:, None, None, None] == jnp.arange(4, dtype=jnp.int32)[None, None, :, None]
    tr = jnp.where(hot, transfer[:, :, None, :], jnp.zeros((), BF16)).reshape(
        LEAVES * RANK, LANES
    )
    vmem = lambda shape, dtype=BF16: pltpu.VMEM(shape, dtype)
    dma = lambda *shape: pltpu.SemaphoreType.DMA(shape)
    anywhere = pl.BlockSpec(memory_space=pltpu.HBM)
    smem = pl.BlockSpec(memory_space=pltpu.SMEM)
    whole = pl.BlockSpec(memory_space=pltpu.VMEM)
    return pl.pallas_call(
        kernel,
        out_shape=[jax.ShapeDtypeStruct(vectors.shape, BF16)] * 2,
        in_specs=[smem, smem] + [anywhere] * 7,
        out_specs=[whole] * 2,
        scratch_shapes=[
            vmem((COLS, LEAVES * LEAF)),
            vmem((LEAVES, 2, LEAF, LEAF)),
            vmem((LEAVES * RANK, LEAF)),
            vmem((LEAVES * RANK, FAR * RANK)),
            vmem((LEAVES * RANK, LANES)),
            vmem((4 * RANK, CLUS * RANK)),
            vmem((CLUS, COLS, LANES)),
            vmem((RHS, 3 * LEAVES, COLS, LEAF)),
            vmem((RHS, 3 * LEAVES, COLS, LEAF)),
            vmem((2, RHS, LEAVES, COLS, LEAF)),
            vmem((2, 2, LEAVES, COLS, LEAF)),
            vmem((2, LEAVES, COLS, LEAF)),
            vmem((EMPTY + 1, COLS, LANES), F32),
            vmem((LEAVES, COLS, LEAF), F32),
            vmem((2, CLUS, COLS, LANES)),
            vmem((2, CLUS, COLS, LANES)),
            vmem((2, COLS, LANES), F32),
            vmem((2, 3, COLS, LANES), F32),
            vmem((2, COLS, LANES)),
            vmem((2, CLUS // 4, COLS, LANES)),
            vmem((2, COLS, LANES)),
            vmem((2, 2, COLS, LANES)),
            dma(10),
            dma(2, 3, GROUPS), dma(2, 3, GROUPS),
            dma(2, 2, RHS, GROUPS), dma(2, 2, RHS, GROUPS),
            dma(2, 2, GROUPS), dma(2, 2, GROUPS),
            dma(2, GROUPS), dma(2, GROUPS),
            dma(2), dma(2),
            pltpu.SemaphoreType.DMA, pltpu.SemaphoreType.DMA,
            dma(2, 3), dma(2, 3),
            dma(2), dma(2),
            dma(2, 2), dma(2, 2),
        ],
        compiler_params=pltpu.CompilerParams(
            collective_id=0, has_side_effects=True, vmem_limit_bytes=40 * 1024 * 1024
        ),
    )(
        near_lists, source,
        vectors, near_field_tiles,
        leaf_basis_set.reshape(LEAVES * RANK, LEAF),
        far_coupling.reshape(LEAVES * RANK, FAR * RANK),
        tr, top_coupling, ids,
    )


def solution(mesh):
    placed = (
        P("rhs", "clus"),
        P("clus", "rhs", None, None),
        P("clus", "rhs"),
        P("clus", None, None),
        P("clus", None, None),
        P("clus", None),
        P("clus", None),
        P("clus", None, None),
        P("clus"),
        P("clus", None),
    )
    return jax.shard_map(
        on_device,
        mesh=mesh,
        in_specs=placed,
        out_specs=(P("rhs", "clus"), P("rhs", "clus")),
        check_vma=False,
    )
```

```python
import jax
import jax.numpy as jnp
from jax import lax
from jax.experimental import pallas as pl
from jax.experimental.pallas import tpu as pltpu
from jax.sharding import PartitionSpec as P

MESH = pl.DeviceIdType.MESH
BF16 = jnp.bfloat16
F32 = jnp.float32
CLUS, RHS = 64, 4
LEAVES, RANK, LEAF, COLS = 16, 32, 256, 16
FAR, SLOTS, GROUPS = 8, 4, 4
ORDER = (0, 2, 1, 3)
LANES = 128
EMPTY = LEAVES * FAR


def dot_nn(a, b):
    return lax.dot_general(a, b, (((1,), (0,)), ((), ())), preferred_element_type=F32)


def dot_nt(a, b):
    return lax.dot_general(a, b, (((1,), (1,)), ((), ())), preferred_element_type=F32)


VM = 60


def kernel(
    near_s, parent_s, device_v, leaf_v,
    vec_h, tiles_h, basis_h, coup_h, transfer_h, topc_h,
    out1, out2,
    vec, tiles, basis, coup, transfer, tr, topc, codes, padded, source_v, source_s, ids,
    win0, win1, part, rs, relay, rolled, far,
    term_out, term_in, pair_out, pair_in, top_out, top_in, down_out, down_in,
    load_sem, ag_s, ag_r, halo_s, halo_r, rs_s, rs_r, relay_s, relay_r,
    term_s, term_r, id_s, id_r, pair_s, pair_r, top_s, top_r, down_s, down_r,
):
    me = lax.axis_index("clus")
    row = lax.axis_index("rhs")
    right = lax.rem(row + 1, RHS)
    left = lax.rem(row + RHS - 1, RHS)
    opposite = lax.rem(row + 2, RHS)
    sibling = me + 1 - 2 * lax.rem(me, 2)
    above = lax.rem(me + 1, CLUS)
    below = lax.rem(me + CLUS - 1, CLUS)

    def send(src, dst, s, r, device):
        return pltpu.make_async_remote_copy(
            src_ref=src, dst_ref=dst, send_sem=s, recv_sem=r, device_id=device, device_id_type=MESH
        )

    barrier = pltpu.get_barrier_semaphore()

    def greet(o, c):
        pl.semaphore_signal(
            barrier, inc=1, device_id=(lax.rem(me + o, CLUS), row), device_id_type=MESH
        )
        return c

    lax.fori_loop(1, CLUS, greet, 0)
    for o in range(1, RHS):
        pl.semaphore_signal(
            barrier, inc=1, device_id=(me, lax.rem(row + o, RHS)), device_id_type=MESH
        )

    loads = [
        pltpu.make_async_copy(vec_h, vec, load_sem.at[0]),
        pltpu.make_async_copy(basis_h, basis, load_sem.at[1]),
        pltpu.make_async_copy(transfer_h, transfer, load_sem.at[2]),
        pltpu.make_async_copy(coup_h, coup, load_sem.at[3]),
    ]
    for k in range(4):
        loads.append(
            pltpu.make_async_copy(topc_h, topc.at[pl.ds(k * RANK, RANK)], load_sem.at[4 + k])
        )
    loads.append(pltpu.make_async_copy(tiles_h, tiles, load_sem.at[8]))
    for copy in loads:
        copy.start()
    rolled[EMPTY] = jnp.zeros((COLS, LANES), F32)

    lane = lax.broadcasted_iota(jnp.int32, (COLS, LANES), 1) // RANK
    group_row = lax.broadcasted_iota(jnp.int32, (GROUPS * COLS, LANES), 0) // COLS
    group_lane = lax.broadcasted_iota(jnp.int32, (GROUPS * COLS, LANES), 1) // RANK
    diagonal = group_row == group_lane
    zero = jnp.zeros((COLS, LANES), F32)

    padded[...] = jnp.zeros((FAR, LANES), jnp.int32)
    padded[:, 0:LEAVES] = device_v[...] * LEAVES + leaf_v[...]
    rows8 = lax.broadcasted_iota(jnp.int32, (FAR, LANES), 0)
    codes_row = jnp.where(rows8 == 0, padded[...], 0)
    for p in range(1, FAR):
        codes_row += jnp.where(rows8 == p, pltpu.roll(padded[...], LEAVES * p, 1), 0)
    codes_row = jnp.sum(codes_row, axis=0, keepdims=True)
    codes[me] = codes_row

    at = lax.broadcasted_iota(jnp.int32, (CLUS, LANES), 1)
    down_at = lax.broadcasted_iota(jnp.int32, (CLUS, LANES), 0)

    def earlier(mask):
        ones = jnp.where(mask, 1, 0)
        total = ones
        for k in (1, 2, 4, 8, 16, 32, 64):
            total = total + jnp.where(at >= k, pltpu.roll(total, k, 1), 0)
        return total - ones

    mine = (codes_row >> 4) == down_at
    rank = earlier(mine)
    partner = at >> 4
    table = jnp.zeros((CLUS, LANES), jnp.int32)
    for slot in range(SLOTS):
        tile = (at & 15) * FAR + (partner >> 2) * 4 + ((slot - partner) & 3)
        tile = jnp.where(mine & (rank == slot), tile - EMPTY, 0)
        table = jnp.where(at == slot, EMPTY + jnp.sum(tile, axis=1, keepdims=True), table)
    source_v[...] = table
    table_copy = pltpu.make_async_copy(source_v, source_s, load_sem.at[9])
    table_copy.start()

    loads[2].wait()
    spot = lax.broadcasted_iota(jnp.int32, (RANK, LANES), 1)
    same = (spot & (RANK - 1)) == lax.broadcasted_iota(jnp.int32, (RANK, LANES), 0)
    wide = dot_nn(transfer[...], jnp.where(same, 1.0, 0.0).astype(BF16))
    chip_place = lax.rem(me // 2, 2) * 2
    for i in range(LEAVES):
        place = chip_place + (parent_s[i] & 1)
        tr[i * RANK : (i + 1) * RANK, :] = jnp.where(
            (spot >> 5) == place, wide[i * RANK : (i + 1) * RANK], 0.0
        ).astype(BF16)

    loads[0].wait()
    for i in range(LEAVES):
        win0[row, LEAVES + i] = vec[:, i * LEAF : (i + 1) * LEAF]
    loads[1].wait()
    loads[3].wait()
    table_copy.wait()

    pending = []

    def own_chunk(q, chunk):
        win = (win0, win1)[q]
        block = win.at[row, pl.ds(LEAVES + GROUPS * chunk, GROUPS)]
        copies = [
            send(block, block, ag_s.at[q, 0, chunk], ag_r.at[q, 0, chunk], (me, right)),
            send(block, block, ag_s.at[q, 1, chunk], ag_r.at[q, 1, chunk], (me, left)),
        ] + spread(q, 0, row, chunk)
        for copy in copies:
            copy.start()
        pending.extend(copies)

    def spread(q, o, source, chunk):
        win = (win0, win1)[q]
        base = GROUPS * chunk
        block = win.at[source, pl.ds(LEAVES + base, GROUPS)]
        return [
            send(block, win.at[source, pl.ds(base, GROUPS)],
                 halo_s.at[q, 0, o, chunk], halo_r.at[q, 0, o, chunk], (above, row)),
            send(block, win.at[source, pl.ds(2 * LEAVES + base, GROUPS)],
                 halo_s.at[q, 1, o, chunk], halo_r.at[q, 1, o, chunk], (below, row)),
        ]

    for q in range(2):
        win = (win0, win1)[q]
        coeffs = []
        top_sum = zero
        for g in range(GROUPS):
            values = win[row, LEAVES + GROUPS * g : LEAVES + GROUPS * (g + 1)]
            values = values.reshape(GROUPS * COLS, LEAF)
            product = dot_nt(values, basis[g * LANES : (g + 1) * LANES, :])
            product = jnp.where(diagonal, product, 0.0)
            masked = product.astype(BF16)
            coeffs.append(masked)
            joined = product[0:COLS]
            for t in range(1, GROUPS):
                joined = joined + product[t * COLS : (t + 1) * COLS]
            top_sum = top_sum + dot_nn(joined.astype(BF16), tr[g * LANES : (g + 1) * LANES, :])
        pair_out[q] = top_sum
        pair = send(pair_out.at[q], pair_in.at[q], pair_s.at[q], pair_r.at[q], (sibling, row))
        pending.append(pair)
        if q == 1:
            pair.start()

        for g in range(GROUPS):
            terms = dot_nn(coeffs[g], coup[g * LANES : (g + 1) * LANES, :])
            for t in range(GROUPS):
                for half in range(2):
                    tile = terms[t * COLS : (t + 1) * COLS, half * LANES : (half + 1) * LANES]
                    base = (GROUPS * g + t) * FAR + half * 4
                    rolled[base] = tile
                    for k in range(1, 4):
                        rolled[base + k] = pltpu.roll(tile, RANK * k, 1)

        if q == 0:
            pl.semaphore_wait(barrier, CLUS - 1 + RHS - 1)
            pair.start()
            for chunk in ORDER:
                own_chunk(0, chunk)

        def packed(d):
            parts = [rolled[source_s[d, s]] for s in range(SLOTS)]
            low = jnp.where(lane == 0, parts[0], parts[1])
            high = jnp.where(lane == 2, parts[2], parts[3])
            return jnp.where(lane < 2, low, high).astype(BF16)

        def term_copy(d):
            return send(term_out.at[q, d], term_in.at[q, me], term_s.at[q], term_r.at[q], (d, row))

        def id_copy(d):
            return send(codes.at[me], codes.at[me], id_s, id_r, (d, row))

        def term_start(o, c):
            d = lax.rem(me + o, CLUS)
            term_out[q, d] = packed(d)
            term_copy(d).start()
            if q == 0:
                id_copy(d).start()
            return c

        lax.fori_loop(1, CLUS, term_start, 0)
        term_in[q, me] = packed(me)

        pair.wait_recv()
        top_tile = (top_sum + pair_in[q]).astype(BF16)
        top_out[q] = top_tile
        top_in[q, me // 2] = top_tile

        def top_start(o, c):
            send(top_out.at[q], top_in.at[q, me // 2], top_s.at[q], top_r.at[q],
                 (lax.rem(me + 2 * o, CLUS), row)).start()
            return c

        lax.fori_loop(1, CLUS // 2, top_start, 0)

        halos = []
        for chunk in ORDER:
            for side, source in enumerate((left, right)):
                block = win.at[source, pl.ds(LEAVES + GROUPS * chunk, GROUPS)]
                send(block, block, ag_s.at[q, side, chunk], ag_r.at[q, side, chunk],
                     (me, right)).wait_recv()
                more = spread(q, 1 + 2 * side, source, chunk)
                if side == chunk // 2:
                    more.insert(0, send(block, block, ag_s.at[q, 2, chunk], ag_r.at[q, 2, chunk],
                                        (me, (right, left)[side])))
                for copy in more:
                    copy.start()
                pending += more
        for chunk in ORDER:
            block = win.at[opposite, pl.ds(LEAVES + GROUPS * chunk, GROUPS)]
            send(block, block, ag_s.at[q, 2, chunk], ag_r.at[q, 2, chunk], (me, right)).wait_recv()
            more = spread(q, 2, opposite, chunk)
            for copy in more:
                copy.start()
            pending += more

        if q == 0:
            for k in range(4):
                loads[4 + k].wait()
        pltpu.make_async_copy(
            top_in.at[q, pl.ds(0, CLUS // 2 - 1)], top_in.at[q, pl.ds(0, CLUS // 2 - 1)], top_r.at[q]
        ).wait()
        pairs = CLUS // 4
        tops = [None] * pairs
        for m in range(pairs):
            tops[(m + pairs // 2) % pairs] = top_in[q, 2 * m] + top_in[q, 2 * m + 1]
        local = dot_nt(jnp.concatenate(tops, axis=1), topc[...])
        down_out[q] = jnp.where(lane == lax.rem(me, 4), local, 0.0).astype(BF16)
        across = lax.rem(me + CLUS // 2, CLUS)
        for k, d in enumerate((across, across + 1 - 2 * lax.rem(across, 2))):
            copy = send(down_out.at[q], down_in.at[q, k],
                        down_s.at[q, k], down_r.at[q, k], (d, row))
            copy.start()
            pending.append(copy)
        downs = pending[-2:]

        for chunk in ORDER:
            for o, source in ((0, row), (1, left), (3, right), (2, opposite)):
                for copy in spread(q, o, source, chunk):
                    copy.wait_recv()
        if q == 0:
            loads[8].wait()

        def relay_copy(chunk):
            leaves = pl.ds(chunk * GROUPS, GROUPS)
            return send(part.at[q, opposite, leaves], relay.at[q, leaves],
                        relay_s.at[q, chunk], relay_r.at[q, chunk],
                        (me, (right, left)[chunk // 2]))

        def rs_copy(chunk, side):
            leaves = pl.ds(chunk * GROUPS, GROUPS)
            target = (right, left)[side]
            return send(part.at[q, target, leaves], rs.at[q, side, leaves],
                        rs_s.at[q, side, chunk], rs_r.at[q, side, chunk], (me, target))

        def near_chunk(chunk):
            for n in range(GROUPS):
                leaf = chunk * GROUPS + n
                total = None
                for p in range(2):
                    j = near_s[p, leaf]
                    slot = lax.rem(j - me * LEAVES + LEAVES + CLUS * LEAVES, CLUS * LEAVES)
                    slot = jnp.minimum(slot, 3 * LEAVES - 1)
                    block = win[:, slot].reshape(RHS * COLS, LEAF)
                    product = dot_nt(block, tiles[leaf, p])
                    total = product if total is None else total + product
                for a in range(RHS):
                    part[q, a, leaf] = total[a * COLS : (a + 1) * COLS].astype(BF16)
            copies = (relay_copy(chunk), rs_copy(chunk, 1 - chunk // 2))
            for copy in copies:
                copy.start()
            pending.extend(copies)

        for chunk in ORDER:
            near_chunk(chunk)
        for chunk in ORDER:
            relay_copy(chunk).wait_recv()
            side = chunk // 2
            target = (right, left)[side]
            for n in range(GROUPS):
                leaf = chunk * GROUPS + n
                part[q, target, leaf] = (
                    part[q, target, leaf].astype(F32) + relay[q, leaf].astype(F32)
                ).astype(BF16)
            copy = rs_copy(chunk, side)
            copy.start()
            pending.append(copy)

        pltpu.make_async_copy(
            term_in.at[q, pl.ds(0, CLUS - 1)], term_in.at[q, pl.ds(0, CLUS - 1)], term_r.at[q]
        ).wait()
        if q == 0:
            pltpu.make_async_copy(
                codes.at[pl.ds(0, CLUS - 1)], codes.at[pl.ds(0, CLUS - 1)], id_r
            ).wait()
            arrived = codes[...].reshape(CLUS, LANES)
            mine = (arrived >> 4) == me
            rank = earlier(mine)
            table = jnp.zeros((CLUS, LANES), jnp.int32)
            for slot in range(SLOTS):
                target = jnp.where(mine & (rank == slot), (arrived & 15) + 1, 0)
                table = jnp.where((at >> 5) == slot, jnp.sum(target, axis=1, keepdims=True), table)
            ids[...] = table

        def add_terms(s, sums):
            values = term_in[q, s].astype(F32)
            targets = jnp.broadcast_to(ids[pl.ds(s, 1), :], (COLS, LANES))
            return tuple(
                sums[t] + jnp.where(targets == t + 1, values, 0.0) for t in range(LEAVES)
            )

        sums = lax.fori_loop(0, CLUS, add_terms, (zero,) * LEAVES)

        for copy in downs:
            copy.wait_recv()
        chosen = down_in[q, 0] + down_in[q, 1]
        for g in range(GROUPS):
            down = dot_nt(chosen, tr[g * LANES : (g + 1) * LANES, :])
            rows = []
            for t in range(GROUPS):
                x = sums[GROUPS * g + t]
                x = x + pltpu.roll(x, 2 * RANK, 1)
                x = x + pltpu.roll(x, RANK, 1)
                rows.append(jnp.where(lane == t, x + down, 0.0).astype(BF16))
            result = dot_nn(jnp.concatenate(rows, axis=0), basis[g * LANES : (g + 1) * LANES, :])
            for t in range(GROUPS):
                far[GROUPS * g + t] = result[t * COLS : (t + 1) * COLS]

        out = out1 if q == 0 else out2
        for chunk in ORDER:
            rs_copy(chunk, 1 - chunk // 2).wait_recv()
            rs_copy(chunk, chunk // 2).wait_recv()
            for n in range(GROUPS):
                leaf = chunk * GROUPS + n
                total = far[leaf] + part[q, row, leaf].astype(F32)
                total = total + rs[q, 0, leaf].astype(F32) + rs[q, 1, leaf].astype(F32)
                value = total.astype(BF16)
                out[:, leaf * LEAF : (leaf + 1) * LEAF] = value
                if q == 0:
                    win1[row, LEAVES + leaf] = value
            if q == 0:
                own_chunk(1, chunk)

    for copy in pending:
        copy.wait_send()
    for q in range(2):
        pltpu.make_async_copy(
            top_in.at[q, pl.ds(0, CLUS // 2 - 1)], top_in.at[q, pl.ds(0, CLUS // 2 - 1)], top_s.at[q]
        ).wait()
        pltpu.make_async_copy(
            term_in.at[q, pl.ds(0, CLUS - 1)], term_in.at[q, pl.ds(0, CLUS - 1)], term_s.at[q]
        ).wait()
    pltpu.make_async_copy(
        codes.at[pl.ds(0, CLUS - 1)], codes.at[pl.ds(0, CLUS - 1)], id_s
    ).wait()


def on_device(
    vectors, near_field_tiles, near_lists, leaf_basis_set, far_coupling,
    far_device, far_leaf, transfer, parent, top_coupling,
):
    vmem = lambda shape, dtype=BF16: pltpu.VMEM(shape, dtype)
    dma = lambda *shape: pltpu.SemaphoreType.DMA(shape)
    anywhere = pl.BlockSpec(memory_space=pltpu.HBM)
    smem = pl.BlockSpec(memory_space=pltpu.SMEM)
    whole = pl.BlockSpec(memory_space=pltpu.VMEM)
    return pl.pallas_call(
        kernel,
        out_shape=[jax.ShapeDtypeStruct(vectors.shape, BF16)] * 2,
        in_specs=[smem, smem, whole, whole] + [anywhere] * 6,
        out_specs=[whole] * 2,
        scratch_shapes=[
            vmem((COLS, LEAVES * LEAF)),
            vmem((LEAVES, 2, LEAF, LEAF)),
            vmem((LEAVES * RANK, LEAF)),
            vmem((LEAVES * RANK, FAR * RANK)),
            vmem((LEAVES * RANK, RANK)),
            vmem((LEAVES * RANK, LANES)),
            vmem((4 * RANK, CLUS * RANK)),
            vmem((CLUS, 1, LANES), jnp.int32),
            vmem((FAR, LANES), jnp.int32),
            vmem((CLUS, LANES), jnp.int32),
            pltpu.SMEM((CLUS, LANES), jnp.int32),
            vmem((CLUS, LANES), jnp.int32),
            vmem((RHS, 3 * LEAVES, COLS, LEAF)),
            vmem((RHS, 3 * LEAVES, COLS, LEAF)),
            vmem((2, RHS, LEAVES, COLS, LEAF)),
            vmem((2, 2, LEAVES, COLS, LEAF)),
            vmem((2, LEAVES, COLS, LEAF)),
            vmem((EMPTY + 1, COLS, LANES), F32),
            vmem((LEAVES, COLS, LEAF), F32),
            vmem((2, CLUS, COLS, LANES)),
            vmem((2, CLUS, COLS, LANES)),
            vmem((2, COLS, LANES), F32),
            vmem((2, COLS, LANES), F32),
            vmem((2, COLS, LANES)),
            vmem((2, CLUS // 2, COLS, LANES)),
            vmem((2, COLS, LANES)),
            vmem((2, 2, COLS, LANES)),
            dma(10),
            dma(2, 3, GROUPS), dma(2, 3, GROUPS),
            dma(2, 2, RHS, GROUPS), dma(2, 2, RHS, GROUPS),
            dma(2, 2, GROUPS), dma(2, 2, GROUPS),
            dma(2, GROUPS), dma(2, GROUPS),
            dma(2), dma(2),
            pltpu.SemaphoreType.DMA, pltpu.SemaphoreType.DMA,
            dma(2), dma(2),
            dma(2), dma(2),
            dma(2, 2), dma(2, 2),
        ],
        compiler_params=pltpu.CompilerParams(
            collective_id=0, has_side_effects=True, vmem_limit_bytes=VM * 1024 * 1024
        ),
    )(
        near_lists.T, parent, far_device.T, far_leaf.T,
        vectors, near_field_tiles,
        leaf_basis_set.reshape(LEAVES * RANK, LEAF),
        far_coupling.reshape(LEAVES * RANK, FAR * RANK),
        transfer.reshape(LEAVES * RANK, RANK), top_coupling,
    )


def solution(mesh):
    placed = (
        P("rhs", "clus"),
        P("clus", "rhs", None, None),
        P("clus", "rhs"),
        P("clus", None, None),
        P("clus", None, None),
        P("clus", None),
        P("clus", None),
        P("clus", None, None),
        P("clus"),
        P("clus", None),
    )
    return jax.shard_map(
        on_device,
        mesh=mesh,
        in_specs=placed,
        out_specs=(P("rhs", "clus"), P("rhs", "clus")),
        check_vma=False,
    )
```

```python
import jax
import jax.numpy as jnp
from jax import lax
from jax.experimental import pallas as pl
from jax.experimental.pallas import tpu as pltpu
from jax.sharding import PartitionSpec as P

MESH = pl.DeviceIdType.MESH
BF16 = jnp.bfloat16
F32 = jnp.float32
CLUS, RHS = 64, 4
LEAVES, RANK, LEAF, COLS = 16, 32, 256, 16
FAR, SLOTS, GROUPS = 8, 4, 4
ORDER = (0, 2, 1, 3)
LANES = 128
EMPTY = LEAVES * FAR


def dot_nn(a, b):
    return lax.dot_general(a, b, (((1,), (0,)), ((), ())), preferred_element_type=F32)


def dot_nt(a, b):
    return lax.dot_general(a, b, (((1,), (1,)), ((), ())), preferred_element_type=F32)


VM = 60


def kernel(
    near_s, parent_s, device_v, leaf_v,
    vec_h, tiles_h, basis_h, coup_h, transfer_h, topc_h,
    out1, out2,
    vec, tiles, basis, coup, transfer, tr, own_topc, codes, padded, source_v, source_s, ids,
    win0, win1, part, rs, relay, rolled, far,
    term_out, term_in, pair_out, pair_in, top_out, top_in, down_out, down_in,
    load_sem, ag_s, ag_r, halo_s, halo_r, rs_s, rs_r, relay_s, relay_r,
    term_s, term_r, id_s, id_r, pair_s, pair_r, top_s, top_r, down_s, down_r,
):
    me = lax.axis_index("clus")
    row = lax.axis_index("rhs")
    right = lax.rem(row + 1, RHS)
    left = lax.rem(row + RHS - 1, RHS)
    opposite = lax.rem(row + 2, RHS)
    sibling = me + 1 - 2 * lax.rem(me, 2)
    above = lax.rem(me + 1, CLUS)
    below = lax.rem(me + CLUS - 1, CLUS)

    def send(src, dst, s, r, device):
        return pltpu.make_async_remote_copy(
            src_ref=src, dst_ref=dst, send_sem=s, recv_sem=r, device_id=device, device_id_type=MESH
        )

    barrier = pltpu.get_barrier_semaphore()

    def greet(o, c):
        pl.semaphore_signal(
            barrier, inc=1, device_id=(lax.rem(me + o, CLUS), row), device_id_type=MESH
        )
        return c

    lax.fori_loop(1, CLUS, greet, 0)
    for o in range(1, RHS):
        pl.semaphore_signal(
            barrier, inc=1, device_id=(me, lax.rem(row + o, RHS)), device_id_type=MESH
        )

    loads = [
        pltpu.make_async_copy(vec_h, vec, load_sem.at[0]),
        pltpu.make_async_copy(basis_h, basis, load_sem.at[1]),
        pltpu.make_async_copy(transfer_h, transfer, load_sem.at[2]),
        pltpu.make_async_copy(coup_h, coup, load_sem.at[3]),
    ]
    loads.append(pltpu.make_async_copy(tiles_h, tiles, load_sem.at[4]))
    for k in range(4):
        loads.append(pltpu.make_async_copy(topc_h, own_topc.at[k], load_sem.at[6 + k]))
    for copy in loads:
        copy.start()
    rolled[EMPTY] = jnp.zeros((COLS, LANES), F32)

    lane = lax.broadcasted_iota(jnp.int32, (COLS, LANES), 1) // RANK
    group_row = lax.broadcasted_iota(jnp.int32, (GROUPS * COLS, LANES), 0) // COLS
    group_lane = lax.broadcasted_iota(jnp.int32, (GROUPS * COLS, LANES), 1) // RANK
    diagonal = group_row == group_lane
    zero = jnp.zeros((COLS, LANES), F32)

    padded[...] = jnp.zeros((FAR, LANES), jnp.int32)
    padded[:, 0:LEAVES] = device_v[...] * LEAVES + leaf_v[...]
    rows8 = lax.broadcasted_iota(jnp.int32, (FAR, LANES), 0)
    codes_row = jnp.where(rows8 == 0, padded[...], 0)
    for p in range(1, FAR):
        codes_row += jnp.where(rows8 == p, pltpu.roll(padded[...], LEAVES * p, 1), 0)
    codes_row = jnp.sum(codes_row, axis=0, keepdims=True)
    codes[me] = codes_row

    at = lax.broadcasted_iota(jnp.int32, (CLUS, LANES), 1)
    down_at = lax.broadcasted_iota(jnp.int32, (CLUS, LANES), 0)

    def earlier(mask):
        ones = jnp.where(mask, 1, 0)
        total = ones
        for k in (1, 2, 4, 8, 16, 32, 64):
            total = total + jnp.where(at >= k, pltpu.roll(total, k, 1), 0)
        return total - ones

    mine = (codes_row >> 4) == down_at
    rank = earlier(mine)
    partner = at >> 4
    table = jnp.zeros((CLUS, LANES), jnp.int32)
    for slot in range(SLOTS):
        tile = (at & 15) * FAR + (partner >> 2) * 4 + ((slot - partner) & 3)
        tile = jnp.where(mine & (rank == slot), tile - EMPTY, 0)
        table = jnp.where(at == slot, EMPTY + jnp.sum(tile, axis=1, keepdims=True), table)
    source_v[...] = table
    table_copy = pltpu.make_async_copy(source_v, source_s, load_sem.at[5])
    table_copy.start()

    loads[2].wait()
    spot = lax.broadcasted_iota(jnp.int32, (RANK, LANES), 1)
    same = (spot & (RANK - 1)) == lax.broadcasted_iota(jnp.int32, (RANK, LANES), 0)
    wide = dot_nn(transfer[...], jnp.where(same, 1.0, 0.0).astype(BF16))
    chip_place = lax.rem(me // 2, 2) * 2
    for i in range(LEAVES):
        place = chip_place + (parent_s[i] & 1)
        tr[i * RANK : (i + 1) * RANK, :] = jnp.where(
            (spot >> 5) == place, wide[i * RANK : (i + 1) * RANK], 0.0
        ).astype(BF16)

    loads[0].wait()
    for i in range(LEAVES):
        win0[row, LEAVES + i] = vec[:, i * LEAF : (i + 1) * LEAF]
    loads[1].wait()
    loads[3].wait()
    table_copy.wait()

    across = lax.rem(me + CLUS // 2, CLUS)
    pending = []

    def own_chunk(q, chunk):
        win = (win0, win1)[q]
        block = win.at[row, pl.ds(LEAVES + GROUPS * chunk, GROUPS)]
        copies = [
            send(block, block, ag_s.at[q, 0, chunk], ag_r.at[q, 0, chunk], (me, right)),
            send(block, block, ag_s.at[q, 1, chunk], ag_r.at[q, 1, chunk], (me, left)),
        ] + spread(q, 0, row, chunk)
        for copy in copies:
            copy.start()
        pending.extend(copies)

    def spread(q, o, source, chunk):
        win = (win0, win1)[q]
        base = GROUPS * chunk
        block = win.at[source, pl.ds(LEAVES + base, GROUPS)]
        return [
            send(block, win.at[source, pl.ds(base, GROUPS)],
                 halo_s.at[q, 0, o, chunk], halo_r.at[q, 0, o, chunk], (above, row)),
            send(block, win.at[source, pl.ds(2 * LEAVES + base, GROUPS)],
                 halo_s.at[q, 1, o, chunk], halo_r.at[q, 1, o, chunk], (below, row)),
        ]

    for q in range(2):
        win = (win0, win1)[q]
        coeffs = []
        top_sum = zero
        for g in range(GROUPS):
            values = win[row, LEAVES + GROUPS * g : LEAVES + GROUPS * (g + 1)]
            values = values.reshape(GROUPS * COLS, LEAF)
            product = dot_nt(values, basis[g * LANES : (g + 1) * LANES, :])
            product = jnp.where(diagonal, product, 0.0)
            masked = product.astype(BF16)
            coeffs.append(masked)
            joined = product[0:COLS]
            for t in range(1, GROUPS):
                joined = joined + product[t * COLS : (t + 1) * COLS]
            top_sum = top_sum + dot_nn(joined.astype(BF16), tr[g * LANES : (g + 1) * LANES, :])
        pair_out[q] = top_sum
        pair = send(pair_out.at[q], pair_in.at[q], pair_s.at[q], pair_r.at[q], (sibling, row))
        pending.append(pair)
        if q == 1:
            pair.start()

        for g in range(GROUPS):
            terms = dot_nn(coeffs[g], coup[g * LANES : (g + 1) * LANES, :])
            for t in range(GROUPS):
                for half in range(2):
                    tile = terms[t * COLS : (t + 1) * COLS, half * LANES : (half + 1) * LANES]
                    base = (GROUPS * g + t) * FAR + half * 4
                    rolled[base] = tile
                    for k in range(1, 4):
                        rolled[base + k] = pltpu.roll(tile, RANK * k, 1)

        if q == 0:
            pl.semaphore_wait(barrier, CLUS - 1 + RHS - 1)
            pair.start()
            for chunk in ORDER:
                own_chunk(0, chunk)

        pair.wait_recv()
        top_tile = (top_sum + pair_in[q]).astype(BF16)
        top_out[q] = top_tile
        top_in[q, me // 2] = top_tile

        def top_start(o, c):
            send(top_out.at[q], top_in.at[q, me // 2], top_s.at[q], top_r.at[q],
                 (lax.rem(me + 2 * o, CLUS), row)).start()
            return c

        lax.fori_loop(1, CLUS // 2, top_start, 0)

        def packed(d):
            parts = [rolled[source_s[d, s]] for s in range(SLOTS)]
            low = jnp.where(lane == 0, parts[0], parts[1])
            high = jnp.where(lane == 2, parts[2], parts[3])
            return jnp.where(lane < 2, low, high).astype(BF16)

        def term_copy(d):
            return send(term_out.at[q, d], term_in.at[q, me], term_s.at[q], term_r.at[q], (d, row))

        def id_copy(d):
            return send(codes.at[me], codes.at[me], id_s, id_r, (d, row))

        def term_start(o, c):
            d = lax.rem(me + o, CLUS)
            term_copy(d).start()
            if q == 0:
                id_copy(d).start()
            return c

        def pack(d, c):
            term_out[q, d] = packed(d)
            return c

        lax.fori_loop(0, CLUS, pack, 0)
        term_in[q, me] = term_out[q, me]

        halos = []
        for chunk in ORDER:
            for side, source in enumerate((left, right)):
                block = win.at[source, pl.ds(LEAVES + GROUPS * chunk, GROUPS)]
                send(block, block, ag_s.at[q, side, chunk], ag_r.at[q, side, chunk],
                     (me, right)).wait_recv()
                more = spread(q, 1 + 2 * side, source, chunk)
                if side == chunk // 2:
                    more.insert(0, send(block, block, ag_s.at[q, 2, chunk], ag_r.at[q, 2, chunk],
                                        (me, (right, left)[side])))
                for copy in more:
                    copy.start()
                pending += more
        for chunk in ORDER:
            block = win.at[opposite, pl.ds(LEAVES + GROUPS * chunk, GROUPS)]
            send(block, block, ag_s.at[q, 2, chunk], ag_r.at[q, 2, chunk], (me, right)).wait_recv()
            more = spread(q, 2, opposite, chunk)
            for copy in more:
                copy.start()
            pending += more

        def top_level(rows):
            pltpu.make_async_copy(
                top_in.at[q, pl.ds(0, CLUS // 2 - 1)], top_in.at[q, pl.ds(0, CLUS // 2 - 1)], top_r.at[q]
            ).wait()
            pairs = CLUS // 4
            tops = [None] * pairs
            for m in range(pairs):
                tops[(m + pairs // 2) % pairs] = top_in[q, 2 * m] + top_in[q, 2 * m + 1]
            return dot_nt(
                jnp.concatenate(tops, axis=1), rows[...].reshape(4 * RANK, CLUS * RANK)
            )

        downs = []

        def owner_block():
            if q == 0:
                for copy in loads[5:]:
                    copy.wait()
            local = top_level(own_topc)
            down_out[q] = jnp.where(lane == lax.rem(me, 4), local, 0.0).astype(BF16)
            for k, d in enumerate((across, across + 1 - 2 * lax.rem(across, 2))):
                copy = send(down_out.at[q], down_in.at[q, k], down_s.at[q, k], down_r.at[q, k],
                            (d, row))
                copy.start()
                downs.append(copy)
            pending.extend(downs)

        owner_block()
        lax.fori_loop(1, CLUS, term_start, 0)

        for chunk in ORDER:
            for o, source in ((0, row), (1, left), (3, right), (2, opposite)):
                for copy in spread(q, o, source, chunk):
                    copy.wait_recv()
        if q == 0:
            loads[4].wait()

        def relay_copy(chunk):
            leaves = pl.ds(chunk * GROUPS, GROUPS)
            return send(part.at[q, opposite, leaves], relay.at[q, leaves],
                        relay_s.at[q, chunk], relay_r.at[q, chunk],
                        (me, (right, left)[chunk // 2]))

        def rs_copy(chunk, side):
            leaves = pl.ds(chunk * GROUPS, GROUPS)
            target = (right, left)[side]
            return send(part.at[q, target, leaves], rs.at[q, side, leaves],
                        rs_s.at[q, side, chunk], rs_r.at[q, side, chunk], (me, target))

        def near_chunk(chunk):
            for n in range(GROUPS):
                leaf = chunk * GROUPS + n
                total = None
                for p in range(2):
                    j = near_s[p, leaf]
                    slot = lax.rem(j - me * LEAVES + LEAVES + CLUS * LEAVES, CLUS * LEAVES)
                    slot = jnp.minimum(slot, 3 * LEAVES - 1)
                    block = win[:, slot].reshape(RHS * COLS, LEAF)
                    product = dot_nt(block, tiles[leaf, p])
                    total = product if total is None else total + product
                for a in range(RHS):
                    part[q, a, leaf] = total[a * COLS : (a + 1) * COLS].astype(BF16)
            copies = (relay_copy(chunk), rs_copy(chunk, 1 - chunk // 2))
            for copy in copies:
                copy.start()
            pending.extend(copies)

        for chunk in ORDER:
            near_chunk(chunk)
        for chunk in ORDER:
            relay_copy(chunk).wait_recv()
            side = chunk // 2
            target = (right, left)[side]
            for n in range(GROUPS):
                leaf = chunk * GROUPS + n
                part[q, target, leaf] = (
                    part[q, target, leaf].astype(F32) + relay[q, leaf].astype(F32)
                ).astype(BF16)
            copy = rs_copy(chunk, side)
            copy.start()
            pending.append(copy)

        pltpu.make_async_copy(
            term_in.at[q, pl.ds(0, CLUS - 1)], term_in.at[q, pl.ds(0, CLUS - 1)], term_r.at[q]
        ).wait()
        if q == 0:
            pltpu.make_async_copy(
                codes.at[pl.ds(0, CLUS - 1)], codes.at[pl.ds(0, CLUS - 1)], id_r
            ).wait()
            arrived = codes[...].reshape(CLUS, LANES)
            mine = (arrived >> 4) == me
            rank = earlier(mine)
            table = jnp.zeros((CLUS, LANES), jnp.int32)
            for slot in range(SLOTS):
                target = jnp.where(mine & (rank == slot), (arrived & 15) + 1, 0)
                table = jnp.where((at >> 5) == slot, jnp.sum(target, axis=1, keepdims=True), table)
            ids[...] = table

        def add_terms(s, sums):
            values = term_in[q, s].astype(F32)
            targets = jnp.broadcast_to(ids[pl.ds(s, 1), :], (COLS, LANES))
            return tuple(
                sums[t] + jnp.where(targets == t + 1, values, 0.0) for t in range(LEAVES)
            )

        sums = lax.fori_loop(0, CLUS, add_terms, (zero,) * LEAVES)

        for copy in downs:
            copy.wait_recv()
        chosen = down_in[q, 0] + down_in[q, 1]
        for g in range(GROUPS):
            down = dot_nt(chosen, tr[g * LANES : (g + 1) * LANES, :])
            rows = []
            for t in range(GROUPS):
                x = sums[GROUPS * g + t]
                x = x + pltpu.roll(x, 2 * RANK, 1)
                x = x + pltpu.roll(x, RANK, 1)
                rows.append(jnp.where(lane == t, x + down, 0.0).astype(BF16))
            result = dot_nn(jnp.concatenate(rows, axis=0), basis[g * LANES : (g + 1) * LANES, :])
            for t in range(GROUPS):
                far[GROUPS * g + t] = result[t * COLS : (t + 1) * COLS]

        out = out1 if q == 0 else out2
        for chunk in ORDER:
            rs_copy(chunk, 1 - chunk // 2).wait_recv()
            rs_copy(chunk, chunk // 2).wait_recv()
            for n in range(GROUPS):
                leaf = chunk * GROUPS + n
                total = far[leaf] + part[q, row, leaf].astype(F32)
                total = total + rs[q, 0, leaf].astype(F32) + rs[q, 1, leaf].astype(F32)
                value = total.astype(BF16)
                out[:, leaf * LEAF : (leaf + 1) * LEAF] = value
                if q == 0:
                    win1[row, LEAVES + leaf] = value
            if q == 0:
                own_chunk(1, chunk)

    for copy in pending:
        copy.wait_send()
    for q in range(2):
        pltpu.make_async_copy(
            top_in.at[q, pl.ds(0, CLUS // 2 - 1)], top_in.at[q, pl.ds(0, CLUS // 2 - 1)], top_s.at[q]
        ).wait()
        pltpu.make_async_copy(
            term_in.at[q, pl.ds(0, CLUS - 1)], term_in.at[q, pl.ds(0, CLUS - 1)], term_s.at[q]
        ).wait()
    pltpu.make_async_copy(
        codes.at[pl.ds(0, CLUS - 1)], codes.at[pl.ds(0, CLUS - 1)], id_s
    ).wait()


def on_device(
    vectors, near_field_tiles, near_lists, leaf_basis_set, far_coupling,
    far_device, far_leaf, transfer, parent, top_coupling,
):
    vmem = lambda shape, dtype=BF16: pltpu.VMEM(shape, dtype)
    dma = lambda *shape: pltpu.SemaphoreType.DMA(shape)
    anywhere = pl.BlockSpec(memory_space=pltpu.HBM)
    smem = pl.BlockSpec(memory_space=pltpu.SMEM)
    whole = pl.BlockSpec(memory_space=pltpu.VMEM)
    return pl.pallas_call(
        kernel,
        out_shape=[jax.ShapeDtypeStruct(vectors.shape, BF16)] * 2,
        in_specs=[smem, smem, whole, whole] + [anywhere] * 6,
        out_specs=[whole] * 2,
        scratch_shapes=[
            vmem((COLS, LEAVES * LEAF)),
            vmem((LEAVES, 2, LEAF, LEAF)),
            vmem((LEAVES * RANK, LEAF)),
            vmem((LEAVES * RANK, FAR * RANK)),
            vmem((LEAVES * RANK, RANK)),
            vmem((LEAVES * RANK, LANES)),
            vmem((4, RANK, CLUS * RANK)),
            vmem((CLUS, 1, LANES), jnp.int32),
            vmem((FAR, LANES), jnp.int32),
            vmem((CLUS, LANES), jnp.int32),
            pltpu.SMEM((CLUS, LANES), jnp.int32),
            vmem((CLUS, LANES), jnp.int32),
            vmem((RHS, 3 * LEAVES, COLS, LEAF)),
            vmem((RHS, 3 * LEAVES, COLS, LEAF)),
            vmem((2, RHS, LEAVES, COLS, LEAF)),
            vmem((2, 2, LEAVES, COLS, LEAF)),
            vmem((2, LEAVES, COLS, LEAF)),
            vmem((EMPTY + 1, COLS, LANES), F32),
            vmem((LEAVES, COLS, LEAF), F32),
            vmem((2, CLUS, COLS, LANES)),
            vmem((2, CLUS, COLS, LANES)),
            vmem((2, COLS, LANES), F32),
            vmem((2, COLS, LANES), F32),
            vmem((2, COLS, LANES)),
            vmem((2, CLUS // 2, COLS, LANES)),
            vmem((2, COLS, LANES)),
            vmem((2, 2, COLS, LANES)),
            dma(10),
            dma(2, 3, GROUPS), dma(2, 3, GROUPS),
            dma(2, 2, RHS, GROUPS), dma(2, 2, RHS, GROUPS),
            dma(2, 2, GROUPS), dma(2, 2, GROUPS),
            dma(2, GROUPS), dma(2, GROUPS),
            dma(2), dma(2),
            pltpu.SemaphoreType.DMA, pltpu.SemaphoreType.DMA,
            dma(2), dma(2),
            dma(2), dma(2),
            dma(2, 2), dma(2, 2),
        ],
        compiler_params=pltpu.CompilerParams(
            collective_id=0, has_side_effects=True, vmem_limit_bytes=VM * 1024 * 1024
        ),
    )(
        near_lists.T, parent, far_device.T, far_leaf.T,
        vectors, near_field_tiles,
        leaf_basis_set.reshape(LEAVES * RANK, LEAF),
        far_coupling.reshape(LEAVES * RANK, FAR * RANK),
        transfer.reshape(LEAVES * RANK, RANK), top_coupling,
    )


def solution(mesh):
    placed = (
        P("rhs", "clus"),
        P("clus", "rhs", None, None),
        P("clus", "rhs"),
        P("clus", None, None),
        P("clus", None, None),
        P("clus", None),
        P("clus", None),
        P("clus", None, None),
        P("clus"),
        P("clus", None),
    )
    return jax.shard_map(
        on_device,
        mesh=mesh,
        in_specs=placed,
        out_specs=(P("rhs", "clus"), P("rhs", "clus")),
        check_vma=False,
    )
```

```python
import jax
import jax.numpy as jnp
from jax import lax
from jax.experimental import pallas as pl
from jax.experimental.pallas import tpu as pltpu
from jax.sharding import PartitionSpec as P

MESH = pl.DeviceIdType.MESH
BF16 = jnp.bfloat16
F32 = jnp.float32
CLUS, RHS = 64, 4
LEAVES, RANK, LEAF, COLS = 16, 32, 256, 16
FAR, SLOTS, GROUPS = 8, 4, 4
ORDER = (0, 2, 1, 3)
LANES = 128
EMPTY = LEAVES * FAR


def dot_nn(a, b):
    return lax.dot_general(a, b, (((1,), (0,)), ((), ())), preferred_element_type=F32)


def dot_nt(a, b):
    return lax.dot_general(a, b, (((1,), (1,)), ((), ())), preferred_element_type=F32)


VM = 60


def kernel(
    near_s, parent_s, device_v, leaf_v,
    vec_h, tiles_h, basis_h, coup_h, transfer_h, topc_h,
    out1, out2,
    vec, tiles, basis, coup, transfer, tr, own_topc, codes, padded, source_v, source_s, ids,
    win0, win1, part, rs, relay, rolled, far,
    term_out, term_in, pair_out, pair_in, top_out, top_in, down_out, down_in,
    load_sem, ag_s, ag_r, halo_s, halo_r, rs_s, rs_r, relay_s, relay_r,
    term_s, term_r, id_s, id_r, pair_s, pair_r, top_s, top_r, down_s, down_r,
):
    me = lax.axis_index("clus")
    row = lax.axis_index("rhs")
    right = lax.rem(row + 1, RHS)
    left = lax.rem(row + RHS - 1, RHS)
    opposite = lax.rem(row + 2, RHS)
    sibling = me + 1 - 2 * lax.rem(me, 2)
    above = lax.rem(me + 1, CLUS)
    below = lax.rem(me + CLUS - 1, CLUS)

    def send(src, dst, s, r, device):
        return pltpu.make_async_remote_copy(
            src_ref=src, dst_ref=dst, send_sem=s, recv_sem=r, device_id=device, device_id_type=MESH
        )

    barrier = pltpu.get_barrier_semaphore()

    def greet(o, c):
        pl.semaphore_signal(
            barrier, inc=1, device_id=(lax.rem(me + o, CLUS), row), device_id_type=MESH
        )
        return c

    lax.fori_loop(1, CLUS, greet, 0)
    for o in range(1, RHS):
        pl.semaphore_signal(
            barrier, inc=1, device_id=(me, lax.rem(row + o, RHS)), device_id_type=MESH
        )

    loads = [
        pltpu.make_async_copy(vec_h, vec, load_sem.at[0]),
        pltpu.make_async_copy(basis_h, basis, load_sem.at[1]),
        pltpu.make_async_copy(transfer_h, transfer, load_sem.at[2]),
        pltpu.make_async_copy(coup_h, coup, load_sem.at[3]),
    ]
    loads.append(pltpu.make_async_copy(tiles_h, tiles, load_sem.at[4]))
    for k in range(4):
        loads.append(pltpu.make_async_copy(topc_h, own_topc.at[k], load_sem.at[6 + k]))
    for copy in loads:
        copy.start()
    rolled[EMPTY] = jnp.zeros((COLS, LANES), F32)

    lane = lax.broadcasted_iota(jnp.int32, (COLS, LANES), 1) // RANK
    group_row = lax.broadcasted_iota(jnp.int32, (GROUPS * COLS, LANES), 0) // COLS
    group_lane = lax.broadcasted_iota(jnp.int32, (GROUPS * COLS, LANES), 1) // RANK
    diagonal = group_row == group_lane
    zero = jnp.zeros((COLS, LANES), F32)

    padded[...] = jnp.zeros((FAR, LANES), jnp.int32)
    padded[:, 0:LEAVES] = device_v[...] * LEAVES + leaf_v[...]
    rows8 = lax.broadcasted_iota(jnp.int32, (FAR, LANES), 0)
    codes_row = jnp.where(rows8 == 0, padded[...], 0)
    for p in range(1, FAR):
        codes_row += jnp.where(rows8 == p, pltpu.roll(padded[...], LEAVES * p, 1), 0)
    codes_row = jnp.sum(codes_row, axis=0, keepdims=True)
    codes[me] = codes_row

    at = lax.broadcasted_iota(jnp.int32, (CLUS, LANES), 1)
    down_at = lax.broadcasted_iota(jnp.int32, (CLUS, LANES), 0)

    def earlier(mask):
        ones = jnp.where(mask, 1, 0)
        total = ones
        for k in (1, 2, 4, 8, 16, 32, 64):
            total = total + jnp.where(at >= k, pltpu.roll(total, k, 1), 0)
        return total - ones

    mine = (codes_row >> 4) == down_at
    rank = earlier(mine)
    partner = at >> 4
    table = jnp.zeros((CLUS, LANES), jnp.int32)
    for slot in range(SLOTS):
        tile = (at & 15) * FAR + (partner >> 2) * 4 + ((slot - partner) & 3)
        tile = jnp.where(mine & (rank == slot), tile - EMPTY, 0)
        table = jnp.where(at == slot, EMPTY + jnp.sum(tile, axis=1, keepdims=True), table)
    source_v[...] = table
    table_copy = pltpu.make_async_copy(source_v, source_s, load_sem.at[5])
    table_copy.start()

    loads[2].wait()
    spot = lax.broadcasted_iota(jnp.int32, (RANK, LANES), 1)
    same = (spot & (RANK - 1)) == lax.broadcasted_iota(jnp.int32, (RANK, LANES), 0)
    wide = dot_nn(transfer[...], jnp.where(same, 1.0, 0.0).astype(BF16))
    chip_place = lax.rem(me // 2, 2) * 2
    for i in range(LEAVES):
        place = chip_place + (parent_s[i] & 1)
        tr[i * RANK : (i + 1) * RANK, :] = jnp.where(
            (spot >> 5) == place, wide[i * RANK : (i + 1) * RANK], 0.0
        ).astype(BF16)

    loads[0].wait()
    for i in range(LEAVES):
        win0[row, LEAVES + i] = vec[:, i * LEAF : (i + 1) * LEAF]
    loads[1].wait()
    loads[3].wait()
    table_copy.wait()

    across = lax.rem(me + CLUS // 2, CLUS)
    pending = []

    def own_chunk(q, chunk):
        win = (win0, win1)[q]
        block = win.at[row, pl.ds(LEAVES + GROUPS * chunk, GROUPS)]
        copies = [
            send(block, block, ag_s.at[q, 0, chunk], ag_r.at[q, 0, chunk], (me, right)),
            send(block, block, ag_s.at[q, 1, chunk], ag_r.at[q, 1, chunk], (me, left)),
        ] + spread(q, 0, row, chunk)
        for copy in copies:
            copy.start()
        pending.extend(copies)

    def spread(q, o, source, chunk):
        win = (win0, win1)[q]
        base = GROUPS * chunk
        block = win.at[source, pl.ds(LEAVES + base, GROUPS)]
        return [
            send(block, win.at[source, pl.ds(base, GROUPS)],
                 halo_s.at[q, 0, o, chunk], halo_r.at[q, 0, o, chunk], (above, row)),
            send(block, win.at[source, pl.ds(2 * LEAVES + base, GROUPS)],
                 halo_s.at[q, 1, o, chunk], halo_r.at[q, 1, o, chunk], (below, row)),
        ]

    for q in range(2):
        win = (win0, win1)[q]
        coeffs = []
        top_sum = zero
        for g in range(GROUPS):
            values = win[row, LEAVES + GROUPS * g : LEAVES + GROUPS * (g + 1)]
            values = values.reshape(GROUPS * COLS, LEAF)
            product = dot_nt(values, basis[g * LANES : (g + 1) * LANES, :])
            product = jnp.where(diagonal, product, 0.0)
            masked = product.astype(BF16)
            coeffs.append(masked)
            joined = product[0:COLS]
            for t in range(1, GROUPS):
                joined = joined + product[t * COLS : (t + 1) * COLS]
            top_sum = top_sum + dot_nn(joined.astype(BF16), tr[g * LANES : (g + 1) * LANES, :])
        pair_out[q] = top_sum
        pair = send(pair_out.at[q], pair_in.at[q], pair_s.at[q], pair_r.at[q], (sibling, row))
        pending.append(pair)
        if q == 1:
            pair.start()

        for g in range(GROUPS):
            terms = dot_nn(coeffs[g], coup[g * LANES : (g + 1) * LANES, :])
            for t in range(GROUPS):
                for half in range(2):
                    tile = terms[t * COLS : (t + 1) * COLS, half * LANES : (half + 1) * LANES]
                    base = (GROUPS * g + t) * FAR + half * 4
                    rolled[base] = tile
                    for k in range(1, 4):
                        rolled[base + k] = pltpu.roll(tile, RANK * k, 1)

        if q == 0:
            pl.semaphore_wait(barrier, CLUS - 1 + RHS - 1)
            pair.start()
            for chunk in ORDER:
                own_chunk(0, chunk)

        pair.wait_recv()
        top_tile = (top_sum + pair_in[q]).astype(BF16)
        top_out[q] = top_tile
        top_in[q, me // 2] = top_tile

        def top_send(d):
            send(top_out.at[q], top_in.at[q, me // 2], top_s.at[q], top_r.at[q], (d, row)).start()

        def top_start(j, c):
            k = 2 * j
            top_send(lax.rem(me + k, CLUS))
            top_send(lax.rem(me + CLUS - k, CLUS))
            return c

        lax.fori_loop(1, CLUS // 4, top_start, 0)
        top_send(across)

        def packed(d):
            parts = [rolled[source_s[d, s]] for s in range(SLOTS)]
            low = jnp.where(lane == 0, parts[0], parts[1])
            high = jnp.where(lane == 2, parts[2], parts[3])
            return jnp.where(lane < 2, low, high).astype(BF16)

        def term_copy(d, g):
            return send(term_out.at[q, d], term_in.at[q, me], term_s.at[q], term_r.at[q, g],
                        (d, row))

        def id_copy(d):
            return send(codes.at[me], codes.at[me], id_s, id_r, (d, row))

        def pack(d, c):
            term_out[q, d] = packed(d)
            return c

        lax.fori_loop(0, CLUS, pack, 0)
        term_in[q, me] = term_out[q, me]

        halos = []
        for chunk in ORDER:
            for side, source in enumerate((left, right)):
                block = win.at[source, pl.ds(LEAVES + GROUPS * chunk, GROUPS)]
                send(block, block, ag_s.at[q, side, chunk], ag_r.at[q, side, chunk],
                     (me, right)).wait_recv()
                more = spread(q, 1 + 2 * side, source, chunk)
                if side == chunk // 2:
                    more.insert(0, send(block, block, ag_s.at[q, 2, chunk], ag_r.at[q, 2, chunk],
                                        (me, (right, left)[side])))
                for copy in more:
                    copy.start()
                pending += more
        for chunk in ORDER:
            block = win.at[opposite, pl.ds(LEAVES + GROUPS * chunk, GROUPS)]
            send(block, block, ag_s.at[q, 2, chunk], ag_r.at[q, 2, chunk], (me, right)).wait_recv()
            more = spread(q, 2, opposite, chunk)
            for copy in more:
                copy.start()
            pending += more

        def top_level(rows):
            pltpu.make_async_copy(
                top_in.at[q, pl.ds(0, CLUS // 2 - 1)], top_in.at[q, pl.ds(0, CLUS // 2 - 1)], top_r.at[q]
            ).wait()
            pairs = CLUS // 4
            tops = [None] * pairs
            for m in range(pairs):
                tops[(m + pairs // 2) % pairs] = top_in[q, 2 * m] + top_in[q, 2 * m + 1]
            return dot_nt(
                jnp.concatenate(tops, axis=1), rows[...].reshape(4 * RANK, CLUS * RANK)
            )

        downs = []

        def owner_block():
            if q == 0:
                for copy in loads[5:]:
                    copy.wait()
            local = top_level(own_topc)
            down_out[q] = jnp.where(lane == lax.rem(me, 4), local, 0.0).astype(BF16)
            for k, d in enumerate((across, across + 1 - 2 * lax.rem(across, 2))):
                copy = send(down_out.at[q], down_in.at[q, k], down_s.at[q, k], down_r.at[q, k],
                            (d, row))
                copy.start()
                downs.append(copy)
            pending.extend(downs)

        owner_block()
        def away(g, j):
            return 8 * g + 1 + j

        def distances(g):
            return 0, (7 if g == GROUPS - 1 else 8)

        single = GROUPS - 1
        for g in range(GROUPS):
            def term_start(j, c):
                k = away(g, j)
                for d in (lax.rem(me + k, CLUS), lax.rem(me + CLUS - k, CLUS)):
                    term_copy(d, g).start()
                    if q == 0:
                        id_copy(d).start()
                return c

            if g == single:
                term_copy(across, g).start()
                if q == 0:
                    id_copy(across).start()
            lax.fori_loop(*distances(g), term_start, 0)

        for chunk in ORDER:
            for o, source in ((0, row), (1, left), (3, right), (2, opposite)):
                for copy in spread(q, o, source, chunk):
                    copy.wait_recv()
        if q == 0:
            loads[4].wait()

        def relay_copy(chunk):
            leaves = pl.ds(chunk * GROUPS, GROUPS)
            return send(part.at[q, opposite, leaves], relay.at[q, leaves],
                        relay_s.at[q, chunk], relay_r.at[q, chunk],
                        (me, (right, left)[chunk // 2]))

        def rs_copy(chunk, side):
            leaves = pl.ds(chunk * GROUPS, GROUPS)
            target = (right, left)[side]
            return send(part.at[q, target, leaves], rs.at[q, side, leaves],
                        rs_s.at[q, side, chunk], rs_r.at[q, side, chunk], (me, target))

        def near_chunk(chunk):
            for n in range(GROUPS):
                leaf = chunk * GROUPS + n
                total = None
                for p in range(2):
                    j = near_s[p, leaf]
                    slot = lax.rem(j - me * LEAVES + LEAVES + CLUS * LEAVES, CLUS * LEAVES)
                    slot = jnp.minimum(slot, 3 * LEAVES - 1)
                    block = win[:, slot].reshape(RHS * COLS, LEAF)
                    product = dot_nt(block, tiles[leaf, p])
                    total = product if total is None else total + product
                for a in range(RHS):
                    part[q, a, leaf] = total[a * COLS : (a + 1) * COLS].astype(BF16)
            copies = (relay_copy(chunk), rs_copy(chunk, 1 - chunk // 2))
            for copy in copies:
                copy.start()
            pending.extend(copies)

        for chunk in ORDER:
            near_chunk(chunk)
        for chunk in ORDER:
            relay_copy(chunk).wait_recv()
            side = chunk // 2
            target = (right, left)[side]
            for n in range(GROUPS):
                leaf = chunk * GROUPS + n
                part[q, target, leaf] = (
                    part[q, target, leaf].astype(F32) + relay[q, leaf].astype(F32)
                ).astype(BF16)
            copy = rs_copy(chunk, side)
            copy.start()
            pending.append(copy)

        if q == 0:
            pltpu.make_async_copy(
                codes.at[pl.ds(0, CLUS - 1)], codes.at[pl.ds(0, CLUS - 1)], id_r
            ).wait()
            arrived = codes[...].reshape(CLUS, LANES)
            mine = (arrived >> 4) == me
            rank = earlier(mine)
            table = jnp.zeros((CLUS, LANES), jnp.int32)
            for slot in range(SLOTS):
                target = jnp.where(mine & (rank == slot), (arrived & 15) + 1, 0)
                table = jnp.where((at >> 5) == slot, jnp.sum(target, axis=1, keepdims=True), table)
            ids[...] = table

        def add_terms(s, sums):
            values = term_in[q, s].astype(F32)
            targets = jnp.broadcast_to(ids[pl.ds(s, 1), :], (COLS, LANES))
            return tuple(
                sums[t] + jnp.where(targets == t + 1, values, 0.0) for t in range(LEAVES)
            )

        sums = add_terms(me, (zero,) * LEAVES)
        for g in range(GROUPS):
            def add_both(j, sums):
                k = away(g, j)
                sums = add_terms(lax.rem(me + k, CLUS), sums)
                return add_terms(lax.rem(me + CLUS - k, CLUS), sums)

            low, high = distances(g)
            count = 2 * (high - low) + (1 if g == single else 0)
            pltpu.make_async_copy(
                term_in.at[q, pl.ds(0, count)], term_in.at[q, pl.ds(0, count)], term_r.at[q, g]
            ).wait()
            if g == single:
                sums = add_terms(across, sums)
            sums = lax.fori_loop(low, high, add_both, sums)

        for copy in downs:
            copy.wait_recv()
        chosen = down_in[q, 0] + down_in[q, 1]
        for g in range(GROUPS):
            down = dot_nt(chosen, tr[g * LANES : (g + 1) * LANES, :])
            rows = []
            for t in range(GROUPS):
                x = sums[GROUPS * g + t]
                x = x + pltpu.roll(x, 2 * RANK, 1)
                x = x + pltpu.roll(x, RANK, 1)
                rows.append(jnp.where(lane == t, x + down, 0.0).astype(BF16))
            result = dot_nn(jnp.concatenate(rows, axis=0), basis[g * LANES : (g + 1) * LANES, :])
            for t in range(GROUPS):
                far[GROUPS * g + t] = result[t * COLS : (t + 1) * COLS]

        out = out1 if q == 0 else out2
        for chunk in ORDER:
            rs_copy(chunk, 1 - chunk // 2).wait_recv()
            rs_copy(chunk, chunk // 2).wait_recv()
            for n in range(GROUPS):
                leaf = chunk * GROUPS + n
                total = far[leaf] + part[q, row, leaf].astype(F32)
                total = total + rs[q, 0, leaf].astype(F32) + rs[q, 1, leaf].astype(F32)
                value = total.astype(BF16)
                out[:, leaf * LEAF : (leaf + 1) * LEAF] = value
                if q == 0:
                    win1[row, LEAVES + leaf] = value
            if q == 0:
                own_chunk(1, chunk)

    for copy in pending:
        copy.wait_send()
    for q in range(2):
        pltpu.make_async_copy(
            top_in.at[q, pl.ds(0, CLUS // 2 - 1)], top_in.at[q, pl.ds(0, CLUS // 2 - 1)], top_s.at[q]
        ).wait()
        pltpu.make_async_copy(
            term_in.at[q, pl.ds(0, CLUS - 1)], term_in.at[q, pl.ds(0, CLUS - 1)], term_s.at[q]
        ).wait()
    pltpu.make_async_copy(
        codes.at[pl.ds(0, CLUS - 1)], codes.at[pl.ds(0, CLUS - 1)], id_s
    ).wait()


def on_device(
    vectors, near_field_tiles, near_lists, leaf_basis_set, far_coupling,
    far_device, far_leaf, transfer, parent, top_coupling,
):
    vmem = lambda shape, dtype=BF16: pltpu.VMEM(shape, dtype)
    dma = lambda *shape: pltpu.SemaphoreType.DMA(shape)
    anywhere = pl.BlockSpec(memory_space=pltpu.HBM)
    smem = pl.BlockSpec(memory_space=pltpu.SMEM)
    whole = pl.BlockSpec(memory_space=pltpu.VMEM)
    return pl.pallas_call(
        kernel,
        out_shape=[jax.ShapeDtypeStruct(vectors.shape, BF16)] * 2,
        in_specs=[smem, smem, whole, whole] + [anywhere] * 6,
        out_specs=[whole] * 2,
        scratch_shapes=[
            vmem((COLS, LEAVES * LEAF)),
            vmem((LEAVES, 2, LEAF, LEAF)),
            vmem((LEAVES * RANK, LEAF)),
            vmem((LEAVES * RANK, FAR * RANK)),
            vmem((LEAVES * RANK, RANK)),
            vmem((LEAVES * RANK, LANES)),
            vmem((4, RANK, CLUS * RANK)),
            vmem((CLUS, 1, LANES), jnp.int32),
            vmem((FAR, LANES), jnp.int32),
            vmem((CLUS, LANES), jnp.int32),
            pltpu.SMEM((CLUS, LANES), jnp.int32),
            vmem((CLUS, LANES), jnp.int32),
            vmem((RHS, 3 * LEAVES, COLS, LEAF)),
            vmem((RHS, 3 * LEAVES, COLS, LEAF)),
            vmem((2, RHS, LEAVES, COLS, LEAF)),
            vmem((2, 2, LEAVES, COLS, LEAF)),
            vmem((2, LEAVES, COLS, LEAF)),
            vmem((EMPTY + 1, COLS, LANES), F32),
            vmem((LEAVES, COLS, LEAF), F32),
            vmem((2, CLUS, COLS, LANES)),
            vmem((2, CLUS, COLS, LANES)),
            vmem((2, COLS, LANES), F32),
            vmem((2, COLS, LANES), F32),
            vmem((2, COLS, LANES)),
            vmem((2, CLUS // 2, COLS, LANES)),
            vmem((2, COLS, LANES)),
            vmem((2, 2, COLS, LANES)),
            dma(10),
            dma(2, 3, GROUPS), dma(2, 3, GROUPS),
            dma(2, 2, RHS, GROUPS), dma(2, 2, RHS, GROUPS),
            dma(2, 2, GROUPS), dma(2, 2, GROUPS),
            dma(2, GROUPS), dma(2, GROUPS),
            dma(2), dma(2, GROUPS),
            pltpu.SemaphoreType.DMA, pltpu.SemaphoreType.DMA,
            dma(2), dma(2),
            dma(2), dma(2),
            dma(2, 2), dma(2, 2),
        ],
        compiler_params=pltpu.CompilerParams(
            collective_id=0, has_side_effects=True, vmem_limit_bytes=VM * 1024 * 1024
        ),
    )(
        near_lists.T, parent, far_device.T, far_leaf.T,
        vectors, near_field_tiles,
        leaf_basis_set.reshape(LEAVES * RANK, LEAF),
        far_coupling.reshape(LEAVES * RANK, FAR * RANK),
        transfer.reshape(LEAVES * RANK, RANK), top_coupling,
    )


def solution(mesh):
    placed = (
        P("rhs", "clus"),
        P("clus", "rhs", None, None),
        P("clus", "rhs"),
        P("clus", None, None),
        P("clus", None, None),
        P("clus", None),
        P("clus", None),
        P("clus", None, None),
        P("clus"),
        P("clus", None),
    )
    return jax.shard_map(
        on_device,
        mesh=mesh,
        in_specs=placed,
        out_specs=(P("rhs", "clus"), P("rhs", "clus")),
        check_vma=False,
    )
```

```python
import jax
import jax.numpy as jnp
from jax import lax
from jax.experimental import pallas as pl
from jax.experimental.pallas import tpu as pltpu
from jax.sharding import PartitionSpec as P

MESH = pl.DeviceIdType.MESH
BF16 = jnp.bfloat16
F32 = jnp.float32
CLUS, RHS = 64, 4
LEAVES, RANK, LEAF, COLS = 16, 32, 256, 16
FAR, SLOTS, GROUPS = 8, 4, 4
ORDER = (0, 2, 1, 3)
LANES = 128
EMPTY = LEAVES * FAR


def dot_nn(a, b):
    return lax.dot_general(a, b, (((1,), (0,)), ((), ())), preferred_element_type=F32)


def dot_nt(a, b):
    return lax.dot_general(a, b, (((1,), (1,)), ((), ())), preferred_element_type=F32)


VM = 60


def kernel(
    near_s, parent_s, device_v, leaf_v,
    vec_h, tiles_h, basis_h, coup_h, transfer_h, topc_h,
    both,
    vec, tiles, basis, coup, transfer, tr, own_topc, codes, padded, source_v, source_s, ids,
    win0, win1, part, rs, relay, rolled, far,
    term_out, term_in, pair_out, pair_in, top_out, top_in, down_out, down_in,
    load_sem, ag_s, ag_r, halo_s, halo_r, rs_s, rs_r, relay_s, relay_r,
    term_s, term_r, id_s, id_r, pair_s, pair_r, top_s, top_r, down_s, down_r,
):
    me = lax.axis_index("clus")
    row = lax.axis_index("rhs")
    right = lax.rem(row + 1, RHS)
    left = lax.rem(row + RHS - 1, RHS)
    opposite = lax.rem(row + 2, RHS)
    sibling = me + 1 - 2 * lax.rem(me, 2)
    above = lax.rem(me + 1, CLUS)
    below = lax.rem(me + CLUS - 1, CLUS)

    def send(src, dst, s, r, device):
        return pltpu.make_async_remote_copy(
            src_ref=src, dst_ref=dst, send_sem=s, recv_sem=r, device_id=device, device_id_type=MESH
        )

    barrier = pltpu.get_barrier_semaphore()

    def greet(o, c):
        pl.semaphore_signal(
            barrier, inc=1, device_id=(lax.rem(me + o, CLUS), row), device_id_type=MESH
        )
        return c

    lax.fori_loop(1, CLUS, greet, 0)
    for o in range(1, RHS):
        pl.semaphore_signal(
            barrier, inc=1, device_id=(me, lax.rem(row + o, RHS)), device_id_type=MESH
        )

    loads = [
        pltpu.make_async_copy(vec_h, vec, load_sem.at[0]),
        pltpu.make_async_copy(basis_h, basis, load_sem.at[1]),
        pltpu.make_async_copy(transfer_h, transfer, load_sem.at[2]),
        pltpu.make_async_copy(coup_h, coup, load_sem.at[3]),
    ]
    loads.append(pltpu.make_async_copy(tiles_h, tiles, load_sem.at[4]))
    for k in range(4):
        loads.append(pltpu.make_async_copy(topc_h, own_topc.at[k], load_sem.at[6 + k]))
    for copy in loads:
        copy.start()
    rolled[EMPTY] = jnp.zeros((COLS, LANES), F32)

    lane = lax.broadcasted_iota(jnp.int32, (COLS, LANES), 1) // RANK
    group_row = lax.broadcasted_iota(jnp.int32, (GROUPS * COLS, LANES), 0) // COLS
    group_lane = lax.broadcasted_iota(jnp.int32, (GROUPS * COLS, LANES), 1) // RANK
    diagonal = group_row == group_lane
    zero = jnp.zeros((COLS, LANES), F32)

    padded[...] = jnp.zeros((FAR, LANES), jnp.int32)
    padded[:, 0:LEAVES] = device_v[...] * LEAVES + leaf_v[...]
    rows8 = lax.broadcasted_iota(jnp.int32, (FAR, LANES), 0)
    codes_row = jnp.where(rows8 == 0, padded[...], 0)
    for p in range(1, FAR):
        codes_row += jnp.where(rows8 == p, pltpu.roll(padded[...], LEAVES * p, 1), 0)
    codes_row = jnp.sum(codes_row, axis=0, keepdims=True)
    codes[me] = codes_row

    at = lax.broadcasted_iota(jnp.int32, (CLUS, LANES), 1)
    down_at = lax.broadcasted_iota(jnp.int32, (CLUS, LANES), 0)

    def earlier(mask):
        ones = jnp.where(mask, 1, 0)
        total = ones
        for k in (1, 2, 4, 8, 16, 32, 64):
            total = total + jnp.where(at >= k, pltpu.roll(total, k, 1), 0)
        return total - ones

    mine = (codes_row >> 4) == down_at
    rank = earlier(mine)
    partner = at >> 4
    table = jnp.zeros((CLUS, LANES), jnp.int32)
    for slot in range(SLOTS):
        tile = (at & 15) * FAR + (partner >> 2) * 4 + ((slot - partner) & 3)
        tile = jnp.where(mine & (rank == slot), tile - EMPTY, 0)
        table = jnp.where(at == slot, EMPTY + jnp.sum(tile, axis=1, keepdims=True), table)
    source_v[...] = table
    table_copy = pltpu.make_async_copy(source_v, source_s, load_sem.at[5])
    table_copy.start()

    loads[2].wait()
    spot = lax.broadcasted_iota(jnp.int32, (RANK, LANES), 1)
    same = (spot & (RANK - 1)) == lax.broadcasted_iota(jnp.int32, (RANK, LANES), 0)
    wide = dot_nn(transfer[...], jnp.where(same, 1.0, 0.0).astype(BF16))
    chip_place = lax.rem(me // 2, 2) * 2
    for i in range(LEAVES):
        place = chip_place + (parent_s[i] & 1)
        tr[i * RANK : (i + 1) * RANK, :] = jnp.where(
            (spot >> 5) == place, wide[i * RANK : (i + 1) * RANK], 0.0
        ).astype(BF16)

    loads[0].wait()
    for i in range(LEAVES):
        win0[row, LEAVES + i] = vec[:, i * LEAF : (i + 1) * LEAF]
    loads[1].wait()
    loads[3].wait()
    table_copy.wait()

    across = lax.rem(me + CLUS // 2, CLUS)
    pending = []

    def own_chunk(q, chunk):
        win = (win0, win1)[q]
        block = win.at[row, pl.ds(LEAVES + GROUPS * chunk, GROUPS)]
        copies = [
            send(block, block, ag_s.at[q, 0, chunk], ag_r.at[q, 0, chunk], (me, right)),
            send(block, block, ag_s.at[q, 1, chunk], ag_r.at[q, 1, chunk], (me, left)),
        ] + spread(q, 0, row, chunk)
        for copy in copies:
            copy.start()
        pending.extend(copies)

    def spread(q, o, source, chunk):
        win = (win0, win1)[q]
        base = GROUPS * chunk
        block = win.at[source, pl.ds(LEAVES + base, GROUPS)]
        return [
            send(block, win.at[source, pl.ds(base, GROUPS)],
                 halo_s.at[q, 0, o, chunk], halo_r.at[q, 0, o, chunk], (above, row)),
            send(block, win.at[source, pl.ds(2 * LEAVES + base, GROUPS)],
                 halo_s.at[q, 1, o, chunk], halo_r.at[q, 1, o, chunk], (below, row)),
        ]

    for q in range(2):
        win = (win0, win1)[q]
        coeffs = []
        top_sum = zero
        for g in range(GROUPS):
            values = win[row, LEAVES + GROUPS * g : LEAVES + GROUPS * (g + 1)]
            values = values.reshape(GROUPS * COLS, LEAF)
            product = dot_nt(values, basis[g * LANES : (g + 1) * LANES, :])
            product = jnp.where(diagonal, product, 0.0)
            masked = product.astype(BF16)
            coeffs.append(masked)
            joined = product[0:COLS]
            for t in range(1, GROUPS):
                joined = joined + product[t * COLS : (t + 1) * COLS]
            top_sum = top_sum + dot_nn(joined.astype(BF16), tr[g * LANES : (g + 1) * LANES, :])
        pair_out[q] = top_sum
        pair = send(pair_out.at[q], pair_in.at[q], pair_s.at[q], pair_r.at[q], (sibling, row))
        pending.append(pair)
        if q == 1:
            pair.start()

        for g in range(GROUPS):
            terms = dot_nn(coeffs[g], coup[g * LANES : (g + 1) * LANES, :])
            for t in range(GROUPS):
                for half in range(2):
                    tile = terms[t * COLS : (t + 1) * COLS, half * LANES : (half + 1) * LANES]
                    base = (GROUPS * g + t) * FAR + half * 4
                    rolled[base] = tile
                    for k in range(1, 4):
                        rolled[base + k] = pltpu.roll(tile, RANK * k, 1)

        if q == 0:
            pl.semaphore_wait(barrier, CLUS - 1 + RHS - 1)
            pair.start()
            for chunk in ORDER:
                own_chunk(0, chunk)

        pair.wait_recv()
        top_tile = (top_sum + pair_in[q]).astype(BF16)
        top_out[q] = top_tile
        top_in[q, me // 2] = top_tile

        def top_send(d):
            send(top_out.at[q], top_in.at[q, me // 2], top_s.at[q], top_r.at[q], (d, row)).start()

        def top_start(j, c):
            k = 2 * j
            top_send(lax.rem(me + k, CLUS))
            top_send(lax.rem(me + CLUS - k, CLUS))
            return c

        lax.fori_loop(1, CLUS // 4, top_start, 0)
        top_send(across)

        def packed(d):
            parts = [rolled[source_s[d, s]] for s in range(SLOTS)]
            low = jnp.where(lane == 0, parts[0], parts[1])
            high = jnp.where(lane == 2, parts[2], parts[3])
            return jnp.where(lane < 2, low, high).astype(BF16)

        def term_copy(d, g):
            return send(term_out.at[q, d], term_in.at[q, me], term_s.at[q], term_r.at[q, g],
                        (d, row))

        def id_copy(d):
            return send(codes.at[me], codes.at[me], id_s, id_r, (d, row))

        def pack(d, c):
            term_out[q, d] = packed(d)
            return c

        lax.fori_loop(0, CLUS, pack, 0)
        term_in[q, me] = term_out[q, me]

        halos = []
        for chunk in ORDER:
            for side, source in enumerate((left, right)):
                block = win.at[source, pl.ds(LEAVES + GROUPS * chunk, GROUPS)]
                send(block, block, ag_s.at[q, side, chunk], ag_r.at[q, side, chunk],
                     (me, right)).wait_recv()
                more = spread(q, 1 + 2 * side, source, chunk)
                if side == chunk // 2:
                    more.insert(0, send(block, block, ag_s.at[q, 2, chunk], ag_r.at[q, 2, chunk],
                                        (me, (right, left)[side])))
                for copy in more:
                    copy.start()
                pending += more
        for chunk in ORDER:
            block = win.at[opposite, pl.ds(LEAVES + GROUPS * chunk, GROUPS)]
            send(block, block, ag_s.at[q, 2, chunk], ag_r.at[q, 2, chunk], (me, right)).wait_recv()
            more = spread(q, 2, opposite, chunk)
            for copy in more:
                copy.start()
            pending += more

        def top_level(rows):
            pltpu.make_async_copy(
                top_in.at[q, pl.ds(0, CLUS // 2 - 1)], top_in.at[q, pl.ds(0, CLUS // 2 - 1)], top_r.at[q]
            ).wait()
            pairs = CLUS // 4
            tops = [None] * pairs
            for m in range(pairs):
                tops[(m + pairs // 2) % pairs] = top_in[q, 2 * m] + top_in[q, 2 * m + 1]
            return dot_nt(
                jnp.concatenate(tops, axis=1), rows[...].reshape(4 * RANK, CLUS * RANK)
            )

        downs = []

        def owner_block():
            if q == 0:
                for copy in loads[5:]:
                    copy.wait()
            local = top_level(own_topc)
            down_out[q] = jnp.where(lane == lax.rem(me, 4), local, 0.0).astype(BF16)
            for k, d in enumerate((across, across + 1 - 2 * lax.rem(across, 2))):
                copy = send(down_out.at[q], down_in.at[q, k], down_s.at[q, k], down_r.at[q, k],
                            (d, row))
                copy.start()
                downs.append(copy)
            pending.extend(downs)

        owner_block()
        def away(g, j):
            return 8 * g + 1 + j

        def distances(g):
            return 0, (7 if g == GROUPS - 1 else 8)

        single = GROUPS - 1
        for g in range(GROUPS):
            def term_start(j, c):
                k = away(g, j)
                for d in (lax.rem(me + k, CLUS), lax.rem(me + CLUS - k, CLUS)):
                    term_copy(d, g).start()
                    if q == 0:
                        id_copy(d).start()
                return c

            if g == single:
                term_copy(across, g).start()
                if q == 0:
                    id_copy(across).start()
            lax.fori_loop(*distances(g), term_start, 0)

        for chunk in ORDER:
            for o, source in ((0, row), (1, left), (3, right), (2, opposite)):
                for copy in spread(q, o, source, chunk):
                    copy.wait_recv()
        if q == 0:
            loads[4].wait()

        def relay_copy(chunk):
            leaves = pl.ds(chunk * GROUPS, GROUPS)
            return send(part.at[q, opposite, leaves], relay.at[q, leaves],
                        relay_s.at[q, chunk], relay_r.at[q, chunk],
                        (me, (right, left)[chunk // 2]))

        def rs_copy(chunk, side):
            leaves = pl.ds(chunk * GROUPS, GROUPS)
            target = (right, left)[side]
            return send(part.at[q, target, leaves], rs.at[q, side, leaves],
                        rs_s.at[q, side, chunk], rs_r.at[q, side, chunk], (me, target))

        def near_chunk(chunk):
            for n in range(GROUPS):
                leaf = chunk * GROUPS + n
                total = None
                for p in range(2):
                    j = near_s[p, leaf]
                    slot = lax.rem(j - me * LEAVES + LEAVES + CLUS * LEAVES, CLUS * LEAVES)
                    slot = jnp.minimum(slot, 3 * LEAVES - 1)
                    block = win[:, slot].reshape(RHS * COLS, LEAF)
                    product = dot_nt(block, tiles[leaf, p])
                    total = product if total is None else total + product
                for a in range(RHS):
                    part[q, a, leaf] = total[a * COLS : (a + 1) * COLS].astype(BF16)
            copies = (relay_copy(chunk), rs_copy(chunk, 1 - chunk // 2))
            for copy in copies:
                copy.start()
            pending.extend(copies)

        for chunk in ORDER:
            near_chunk(chunk)
        for chunk in ORDER:
            relay_copy(chunk).wait_recv()
            side = chunk // 2
            target = (right, left)[side]
            for n in range(GROUPS):
                leaf = chunk * GROUPS + n
                part[q, target, leaf] = (
                    part[q, target, leaf].astype(F32) + relay[q, leaf].astype(F32)
                ).astype(BF16)
            copy = rs_copy(chunk, side)
            copy.start()
            pending.append(copy)

        if q == 0:
            pltpu.make_async_copy(
                codes.at[pl.ds(0, CLUS - 1)], codes.at[pl.ds(0, CLUS - 1)], id_r
            ).wait()
            arrived = codes[...].reshape(CLUS, LANES)
            mine = (arrived >> 4) == me
            rank = earlier(mine)
            table = jnp.zeros((CLUS, LANES), jnp.int32)
            for slot in range(SLOTS):
                target = jnp.where(mine & (rank == slot), (arrived & 15) + 1, 0)
                table = jnp.where((at >> 5) == slot, jnp.sum(target, axis=1, keepdims=True), table)
            ids[...] = table

        def add_terms(s, sums):
            values = term_in[q, s].astype(F32)
            targets = jnp.broadcast_to(ids[pl.ds(s, 1), :], (COLS, LANES))
            return tuple(
                sums[t] + jnp.where(targets == t + 1, values, 0.0) for t in range(LEAVES)
            )

        sums = add_terms(me, (zero,) * LEAVES)
        for g in range(GROUPS):
            def add_both(j, sums):
                k = away(g, j)
                sums = add_terms(lax.rem(me + k, CLUS), sums)
                return add_terms(lax.rem(me + CLUS - k, CLUS), sums)

            low, high = distances(g)
            count = 2 * (high - low) + (1 if g == single else 0)
            pltpu.make_async_copy(
                term_in.at[q, pl.ds(0, count)], term_in.at[q, pl.ds(0, count)], term_r.at[q, g]
            ).wait()
            if g == single:
                sums = add_terms(across, sums)
            sums = lax.fori_loop(low, high, add_both, sums)

        for copy in downs:
            copy.wait_recv()
        chosen = down_in[q, 0] + down_in[q, 1]
        for g in range(GROUPS):
            down = dot_nt(chosen, tr[g * LANES : (g + 1) * LANES, :])
            rows = []
            for t in range(GROUPS):
                x = sums[GROUPS * g + t]
                x = x + pltpu.roll(x, 2 * RANK, 1)
                x = x + pltpu.roll(x, RANK, 1)
                rows.append(jnp.where(lane == t, x + down, 0.0).astype(BF16))
            result = dot_nn(jnp.concatenate(rows, axis=0), basis[g * LANES : (g + 1) * LANES, :])
            for t in range(GROUPS):
                far[GROUPS * g + t] = result[t * COLS : (t + 1) * COLS]

        out = both.at[q]
        for chunk in ORDER:
            rs_copy(chunk, 1 - chunk // 2).wait_recv()
            rs_copy(chunk, chunk // 2).wait_recv()
            for n in range(GROUPS):
                leaf = chunk * GROUPS + n
                total = far[leaf] + part[q, row, leaf].astype(F32)
                total = total + rs[q, 0, leaf].astype(F32) + rs[q, 1, leaf].astype(F32)
                value = total.astype(BF16)
                out[:, leaf * LEAF : (leaf + 1) * LEAF] = value
                if q == 0:
                    win1[row, LEAVES + leaf] = value
            if q == 0:
                own_chunk(1, chunk)

    for copy in pending:
        copy.wait_send()
    for q in range(2):
        pltpu.make_async_copy(
            top_in.at[q, pl.ds(0, CLUS // 2 - 1)], top_in.at[q, pl.ds(0, CLUS // 2 - 1)], top_s.at[q]
        ).wait()
        pltpu.make_async_copy(
            term_in.at[q, pl.ds(0, CLUS - 1)], term_in.at[q, pl.ds(0, CLUS - 1)], term_s.at[q]
        ).wait()
    pltpu.make_async_copy(
        codes.at[pl.ds(0, CLUS - 1)], codes.at[pl.ds(0, CLUS - 1)], id_s
    ).wait()


def on_device(
    vectors, near_field_tiles, near_lists, leaf_basis_set, far_coupling,
    far_device, far_leaf, transfer, parent, top_coupling,
):
    vmem = lambda shape, dtype=BF16: pltpu.VMEM(shape, dtype)
    dma = lambda *shape: pltpu.SemaphoreType.DMA(shape)
    anywhere = pl.BlockSpec(memory_space=pltpu.HBM)
    smem = pl.BlockSpec(memory_space=pltpu.SMEM)
    whole = pl.BlockSpec(memory_space=pltpu.VMEM)
    both = pl.pallas_call(
        kernel,
        out_shape=jax.ShapeDtypeStruct((2,) + vectors.shape, BF16),
        in_specs=[smem, smem, whole, whole] + [anywhere] * 6,
        out_specs=whole,
        scratch_shapes=[
            vmem((COLS, LEAVES * LEAF)),
            vmem((LEAVES, 2, LEAF, LEAF)),
            vmem((LEAVES * RANK, LEAF)),
            vmem((LEAVES * RANK, FAR * RANK)),
            vmem((LEAVES * RANK, RANK)),
            vmem((LEAVES * RANK, LANES)),
            vmem((4, RANK, CLUS * RANK)),
            vmem((CLUS, 1, LANES), jnp.int32),
            vmem((FAR, LANES), jnp.int32),
            vmem((CLUS, LANES), jnp.int32),
            pltpu.SMEM((CLUS, LANES), jnp.int32),
            vmem((CLUS, LANES), jnp.int32),
            vmem((RHS, 3 * LEAVES, COLS, LEAF)),
            vmem((RHS, 3 * LEAVES, COLS, LEAF)),
            vmem((2, RHS, LEAVES, COLS, LEAF)),
            vmem((2, 2, LEAVES, COLS, LEAF)),
            vmem((2, LEAVES, COLS, LEAF)),
            vmem((EMPTY + 1, COLS, LANES), F32),
            vmem((LEAVES, COLS, LEAF), F32),
            vmem((2, CLUS, COLS, LANES)),
            vmem((2, CLUS, COLS, LANES)),
            vmem((2, COLS, LANES), F32),
            vmem((2, COLS, LANES), F32),
            vmem((2, COLS, LANES)),
            vmem((2, CLUS // 2, COLS, LANES)),
            vmem((2, COLS, LANES)),
            vmem((2, 2, COLS, LANES)),
            dma(10),
            dma(2, 3, GROUPS), dma(2, 3, GROUPS),
            dma(2, 2, RHS, GROUPS), dma(2, 2, RHS, GROUPS),
            dma(2, 2, GROUPS), dma(2, 2, GROUPS),
            dma(2, GROUPS), dma(2, GROUPS),
            dma(2), dma(2, GROUPS),
            pltpu.SemaphoreType.DMA, pltpu.SemaphoreType.DMA,
            dma(2), dma(2),
            dma(2), dma(2),
            dma(2, 2), dma(2, 2),
        ],
        compiler_params=pltpu.CompilerParams(
            collective_id=0, has_side_effects=True, vmem_limit_bytes=VM * 1024 * 1024
        ),
    )(
        near_lists.T, parent, far_device.T, far_leaf.T,
        vectors, near_field_tiles,
        leaf_basis_set.reshape(LEAVES * RANK, LEAF),
        far_coupling.reshape(LEAVES * RANK, FAR * RANK),
        transfer.reshape(LEAVES * RANK, RANK), top_coupling,
    )
    return both[0], both[1]


def solution(mesh):
    placed = (
        P("rhs", "clus"),
        P("clus", "rhs", None, None),
        P("clus", "rhs"),
        P("clus", None, None),
        P("clus", None, None),
        P("clus", None),
        P("clus", None),
        P("clus", None, None),
        P("clus"),
        P("clus", None),
    )
    return jax.shard_map(
        on_device,
        mesh=mesh,
        in_specs=placed,
        out_specs=(P("rhs", "clus"), P("rhs", "clus")),
        check_vma=False,
    )
```
